256 devices in a mesh: seq: 32 (over y, z_lo, core), tp: 4 (over x), dp: 2 (over z_hi).
Axes of the slice: x: 4, y: 4, z: 8 (z_hi: 2, z_lo: 4; z = z_hi * 4 + z_lo), core: 2. Of those that a mesh axis runs over, the one named last changes fastest.
Arguments:
- frames: bfloat16 [16384, 2048], P(('dp', 'seq')), parts along dimension 0, may hold values from -6 to 6
- w_query: bfloat16 [2048, 2048], P(None, 'tp'), may hold values from -0.70710678 to 0.70710678
- w_key: bfloat16 [2048, 1024], P(None, 'tp'), may hold values from -0.70710678 to 0.70710678
- w_value: bfloat16 [2048, 1024], P(None, 'tp'), may hold values from -0.125 to 0.125
- w_out: bfloat16 [2048, 2048], P('tp'), may hold values from -0.125 to 0.125
- frame_pick: int32 [64, 32, 1], P(('dp', 'seq')), parts along dimension 0, may hold values from 0 to 255
- codes: int32 [2048, 32], P(('dp', 'seq')), parts along dimension 0, may hold values from 0 to 1023
- geo_ids: int32 [2048], P(('dp', 'seq')), parts along dimension 0, may hold values from 0 to 63
- geo_table: bfloat16 [64, 1024], replicated, may hold values from -6 to 6
- w_context: bfloat16 [2048, 1024], P('tp'), may hold values from -0.125 to 0.125
- code_table: bfloat16 [1024, 1024], replicated, may hold values from -6 to 6
- level_table: bfloat16 [32, 1024], replicated, may hold values from -6 to 6
- wd_query: bfloat16 [1024, 1024], P(None, 'tp'), may hold values from -1.25 to 1.25
- wd_key: bfloat16 [1024, 1024], P(None, 'tp'), may hold values from -1.25 to 1.25
- wd_value: bfloat16 [1024, 1024], P(None, 'tp'), may hold values from -0.1875 to 0.1875
- wd_out: bfloat16 [1024, 1024], P('tp'), may hold values from -0.1875 to 0.1875
Outputs:
- temporal: bfloat16 [16384, 2048], P(('dp', 'seq'), 'tp'), parts along dimension 0
- depth: bfloat16 [2048, 32, 1024], P(('dp', 'seq'), None, 'tp'), parts along dimension 0
The draws below stay inside these ranges and needn't reach their ends.
There are 2 independent parts, one for each index of `dp`. The reference program is written for one: setup_inputs(seed, part) draws one part's arguments, and reference() takes and returns one part's arrays. A program takes and returns all parts, laid end to end along the dimension named above; an argument that names none is the same for every part. Nothing has to cross between parts.
All inputs are finite; a program needn't handle non-finite values.
Results may differ from the reference program's by a relative error of at most 0.022.
Values may be sent and summed in bfloat16 or wider, within the bound.
A program may use at most 128 MiB of HBM per device.

```python
import math
import jax
import jax.numpy as jnp
import numpy as np
from jax import lax

D = 2048
HEADS = 16
KV_HEADS = 8
HEAD = 128
DD = 1024
DHEADS = 16
DHEAD = 64
LEVELS = 32
CODEBOOK = 1024
GEO_VOCAB = 64
FR_DEV = 256
FRAMES = 8192
PICK = 1
SLAB = 1024
N_SEQ = 32
N_TP = 4


def scaled_weight(key, rows, columns, fan_in, column_scale):
    values = jax.random.truncated_normal(key, -4.0, 4.0, (rows, columns), jnp.float32)
    return (values * fan_in ** (-0.5) * column_scale[None, :]).astype(jnp.bfloat16)


def draw_w_query(key, part):
    strength = jnp.ones((KV_HEADS,), jnp.float32)
    key = jax.random.fold_in(key, 1)
    column_scale = jnp.repeat(strength, HEADS // KV_HEADS * HEAD)
    return scaled_weight(key, D, D, D, column_scale)


def draw_w_key(key, part):
    strength = jnp.ones((KV_HEADS,), jnp.float32)
    key = jax.random.fold_in(key, 2)
    column_scale = jnp.repeat(strength, HEAD)
    return scaled_weight(key, D, KV_HEADS * HEAD, D, column_scale)


def draw_wd_query(key, part):
    strength = jnp.ones((DHEADS,), jnp.float32)
    key = jax.random.fold_in(key, 3)
    column_scale = jnp.repeat(strength, DHEAD)
    return scaled_weight(key, DD, DD, DD, column_scale)


def draw_wd_key(key, part):
    strength = jnp.ones((DHEADS,), jnp.float32)
    key = jax.random.fold_in(key, 4)
    column_scale = jnp.repeat(strength, DHEAD)
    return scaled_weight(key, DD, DD, DD, column_scale)


def touch_ends(values, own_key, least, top_value):
    longest = values.shape.index(max(values.shape))
    spots = []
    for shift in (0, 1):
        where = [jax.random.randint(jax.random.fold_in(own_key, axis), (), 0, length) for axis, length in enumerate(values.shape)]
        where[longest] = (where[longest] + shift) % values.shape[longest]
        spots.append(tuple(where))
    return values.at[spots[0]].set(least).at[spots[1]].set(top_value)


def block_levels(rng, shape, cuts, smallest, largest):
    def one(dim, shards_of):
        draws = jax.random.uniform(jax.random.fold_in(jax.random.fold_in(rng, 6), dim), (shards_of,), jnp.float32, smallest / len(cuts), largest / len(cuts))
        return jnp.repeat(jnp.exp(draws), shape[dim] // shards_of).reshape((-1,) + (1,) * (len(shape) - dim - 1))

    gain = one(*cuts[0])
    for cut in cuts[1:]:
        gain = gain * one(*cut)
    return gain


def rank_table(number_of, lean):
    weights = [(1 << 20) // math.isqrt(rank ** lean) + 1 for rank in range(1, number_of + 1)]
    scale = 1 + sum(weights) // (1 << 30)
    return np.cumsum(np.array([max(1, weight // scale) for weight in weights]))


def ranked_ids(own_key, extent, number_of, lean):
    grid = rank_table(number_of, lean)
    ticket = jax.random.randint(jax.random.fold_in(own_key, 1), extent, 0, int(grid[number_of - 1]))
    grade = jnp.searchsorted(jnp.asarray(grid, jnp.int32), ticket, side="right")
    return jax.random.permutation(jax.random.fold_in(own_key, 2), number_of)[grade].astype(jnp.int32)


def normal_values(own_key, extent, deviation, reach, split=(), held_as=jnp.bfloat16):
    array = jax.random.normal(own_key, extent, jnp.float32) * deviation
    if len(split) > 0:
        array = block_levels(own_key, extent, split, -0.22, 0.18) * array
    return jnp.clip(array, min=-reach, max=reach).astype(held_as)


def setup_inputs(seed: int = 0, part: int = 0) -> dict:
    key_of = jax.random.split(jax.random.key(seed), 17)
    part_keys = jax.random.split(jax.random.fold_in(key_of[16], part), 17)
    frames = normal_values(part_keys[0], (FRAMES, D), 1.0, 6.0, ((0, 32),))
    w_query = draw_w_query(jax.random.fold_in(key_of[16], 71), part)
    w_key = draw_w_key(jax.random.fold_in(key_of[16], 71), part)
    w_value = normal_values(key_of[3], (D, KV_HEADS * HEAD), D ** -0.5, 0.125, ((1, 4),))
    w_out = normal_values(key_of[4], (D, D), D ** -0.5, 0.125, ((0, 4),))
    frame_pick = touch_ends(jax.random.randint(part_keys[5], (N_SEQ, N_SEQ, PICK), 0, FR_DEV), jax.random.fold_in(part_keys[5], 1), 0, FR_DEV - 1).astype(jnp.int32)
    codes = touch_ends(jax.random.randint(part_keys[6], (SLAB, LEVELS), 0, CODEBOOK), jax.random.fold_in(part_keys[6], 1), 0, CODEBOOK - 1).astype(jnp.int32)
    geo_ids = touch_ends(ranked_ids(part_keys[7], (SLAB,), GEO_VOCAB, 2), jax.random.fold_in(part_keys[7], 3), 0, GEO_VOCAB - 1).astype(jnp.int32)
    geo_table = normal_values(key_of[8], (GEO_VOCAB, DD), 1.0, 6.0)
    w_context = normal_values(key_of[9], (D, DD), D ** -0.5, 0.125, ((0, 4),))
    code_table = normal_values(key_of[10], (CODEBOOK, DD), 1.0, 6.0)
    level_table = normal_values(key_of[11], (LEVELS, DD), 1.0, 6.0)
    wd_query = draw_wd_query(jax.random.fold_in(key_of[16], 71), part)
    wd_key = draw_wd_key(jax.random.fold_in(key_of[16], 71), part)
    wd_value = normal_values(key_of[14], (DD, DD), DD ** -0.5, 0.1875, ((1, 4),))
    wd_out = normal_values(key_of[15], (DD, DD), DD ** -0.5, 0.1875, ((0, 4),))
    return dict(frames=frames, w_query=w_query, w_key=w_key, w_value=w_value, w_out=w_out, frame_pick=frame_pick, codes=codes, geo_ids=geo_ids, geo_table=geo_table, w_context=w_context, code_table=code_table, level_table=level_table, wd_query=wd_query, wd_key=wd_key, wd_value=wd_value, wd_out=wd_out)


def rms_rows(values, epsilon):
    return values * lax.rsqrt(lax.optimization_barrier(jnp.mean(values * values, axis=-1, keepdims=True)) + epsilon)

def temporal_block(queries_block, start, keys_wide, values_wide):
    block = queries_block.shape[0]
    scores = jnp.einsum('qhd,khd->hqk', queries_block, keys_wide) * HEAD ** (-0.5)
    rows_pos = start + jnp.arange(block, dtype=jnp.int32)
    cols_pos = jnp.arange(keys_wide.shape[0], dtype=jnp.int32)
    causal = cols_pos[None, :] <= rows_pos[:, None]
    scores = jnp.where(causal[None], scores, jnp.float32(-1e+30))
    top_score = lax.optimization_barrier(jnp.max(scores, axis=-1, keepdims=True))
    weights = jnp.where(causal[None], jnp.exp(scores - top_score), jnp.float32(0.0))
    totals = lax.optimization_barrier(jnp.sum(weights, axis=-1))
    rounded = lax.optimization_barrier(weights.astype(jnp.bfloat16)).astype(jnp.float32)
    heads_out = jnp.einsum('hqk,khd->qhd', rounded, values_wide) / jnp.transpose(totals)[:, :, None]
    return rms_rows(heads_out, 1e-06).astype(jnp.bfloat16)

def reference(frames, w_query, w_key, w_value, w_out, frame_pick, codes, geo_ids, geo_table, w_context, code_table, level_table, wd_query, wd_key, wd_value, wd_out):
    frames_wide = frames.astype(jnp.float32)
    normed = rms_rows(frames_wide, 1e-05).astype(jnp.bfloat16)
    queries = jnp.dot(normed, w_query, preferred_element_type=jnp.float32).astype(jnp.bfloat16)
    keys_all = jnp.dot(normed, w_key, preferred_element_type=jnp.float32).astype(jnp.bfloat16)
    values_all = jnp.dot(normed, w_value, preferred_element_type=jnp.float32).astype(jnp.bfloat16)
    group = HEADS // KV_HEADS
    keys_wide = jnp.repeat(keys_all.astype(jnp.float32).reshape(FRAMES, KV_HEADS, HEAD), group, axis=1)
    values_wide = jnp.repeat(values_all.astype(jnp.float32).reshape(FRAMES, KV_HEADS, HEAD), group, axis=1)
    blocks = FRAMES // FR_DEV
    queries_blocks = queries.astype(jnp.float32).reshape(blocks, FR_DEV, HEADS, HEAD)
    starts = jnp.arange(blocks, dtype=jnp.int32) * FR_DEV

    def one_block(item):
        return temporal_block(item[0], item[1], keys_wide, values_wide)
    attended = lax.map(one_block, (queries_blocks, starts)).reshape(FRAMES, D)
    temporal = (frames_wide + jnp.dot(attended, w_out, preferred_element_type=jnp.float32)).astype(jnp.bfloat16)
    offsets = jnp.arange(N_SEQ, dtype=jnp.int32) * FR_DEV
    chosen = (jnp.transpose(frame_pick, (1, 0, 2)) + offsets[None, :, None]).reshape(SLAB).astype(jnp.int32)
    picked = jnp.take(temporal, chosen, axis=0)
    context = jnp.dot(picked, w_context, preferred_element_type=jnp.float32).astype(jnp.bfloat16)
    code_rows = jnp.take(code_table, codes[:, :-1], axis=0).astype(jnp.float32)
    code_rows = jnp.concatenate([jnp.zeros((SLAB, 1, DD), jnp.float32), code_rows], axis=1)
    geo_rows = jnp.take(geo_table, geo_ids, axis=0).astype(jnp.float32)
    hidden = context.astype(jnp.float32)[:, None, :] + level_table.astype(jnp.float32)[None] + geo_rows[:, None, :] + code_rows
    depth_normed = rms_rows(hidden, 1e-05).astype(jnp.bfloat16).reshape(SLAB * LEVELS, DD)
    shape_heads = (SLAB, LEVELS, DHEADS, DHEAD)
    depth_queries = jnp.dot(depth_normed, wd_query, preferred_element_type=jnp.float32).astype(jnp.bfloat16).reshape(shape_heads).astype(jnp.float32)
    depth_keys = jnp.dot(depth_normed, wd_key, preferred_element_type=jnp.float32).astype(jnp.bfloat16).reshape(shape_heads).astype(jnp.float32)
    depth_values = jnp.dot(depth_normed, wd_value, preferred_element_type=jnp.float32).astype(jnp.bfloat16).reshape(shape_heads).astype(jnp.float32)
    scores = jnp.einsum('flhd,fmhd->fhlm', depth_queries, depth_keys) * DHEAD ** (-0.5)
    levels_pos = jnp.arange(LEVELS, dtype=jnp.int32)
    causal = levels_pos[None, :] <= levels_pos[:, None]
    scores = jnp.where(causal, scores, jnp.float32(-1e+30))
    top_score = lax.optimization_barrier(jnp.max(scores, axis=-1, keepdims=True))
    weights = jnp.where(causal, jnp.exp(scores - top_score), jnp.float32(0.0))
    totals = lax.optimization_barrier(jnp.sum(weights, axis=-1))
    rounded = lax.optimization_barrier(weights.astype(jnp.bfloat16)).astype(jnp.float32)
    heads_out = jnp.einsum('fhlm,fmhd->flhd', rounded, depth_values) / jnp.transpose(totals, (0, 2, 1))[:, :, :, None]
    depth_attended = rms_rows(heads_out, 1e-06).astype(jnp.bfloat16).reshape(SLAB * LEVELS, DD)
    width_group = DD // N_TP
    summed = jnp.zeros((SLAB * LEVELS, DD), jnp.float32)
    for group_index in range(N_TP):
        lower = group_index * width_group
        part_value = jnp.dot(depth_attended[:, lower:lower + width_group], wd_out[lower:lower + width_group], preferred_element_type=jnp.float32)
        summed = summed + lax.optimization_barrier(part_value.astype(jnp.bfloat16)).astype(jnp.float32)
    depth = (hidden + summed.reshape(SLAB, LEVELS, DD)).astype(jnp.bfloat16)
    return (temporal, depth)
```

```python
import functools
import math

import jax
import jax.numpy as jnp
from jax import lax
from jax.experimental import pallas as pl
from jax.experimental.pallas import tpu as pltpu
from jax.sharding import PartitionSpec as P

MESH = pl.DeviceIdType.MESH
BF16 = jnp.bfloat16
F32 = jnp.float32
LOG2E = math.log2(math.e)

ROWS = 256
D = 2048
HEAD = 128
DD = 1024
DHEAD = 64
LEVELS = 32
SEQ = 32
TP = 4
CHIPS = 16
PAIR = 2 * ROWS
QROWS = 8
DROWS = QROWS * LEVELS
NEG = -1e30

EVENTS = (
    ((0, 0), (0, 1), (1, 0), (0, 2), (1, 1), (0, 3)),
    ((1, 0), (1, 1), (0, 0), (1, 2), (0, 1), (1, 3), (0, 2), (0, 3)),
    ((2, 0), (2, 1), (1, 0), (2, 2), (1, 1), (0, 0), (2, 3), (1, 2), (1, 3), (0, 1), (0, 2), (0, 3)),
    (
        (3, 0), (2, 0), (0, 0), (3, 1), (2, 1), (1, 0), (3, 2), (2, 2),
        (0, 1), (3, 3), (2, 3), (1, 1), (0, 2), (1, 2), (0, 3), (1, 3),
    ),
)
ORDER = ((0, 1, 2, 3), (1, 0, 2, 3), (2, 1, 3, 0), (3, 2, 1, 0))
LEFT, RIGHT, UP, DOWN = range(4)


def pick(index, values):
    out = jnp.int32(values[0])
    for place, value in enumerate(values[1:], 1):
        out = jnp.where(index == place, jnp.int32(value), out)
    return out


def dot(a, b):
    return jnp.dot(a, b, preferred_element_type=F32)


def dot_nt(a, b):
    return lax.dot_general(a, b, (((1,), (1,)), ((), ())), preferred_element_type=F32)


def dot_tn(a, b):
    return lax.dot_general(a, b, (((0,), (0,)), ((), ())), preferred_element_type=F32)


def kernel(
    frames_h, wq_h, wk_h, wv_h, wo_h, pick_ref, codes_ref, geo_ref, geot_ref, wc_h, codet_h, level_ref,
    wdq_h, wdk_h, wdv_h, wdo_h,
    temporal_h, depth_h,
    frames, normed, wqkv, st, q_all, kv, m_s, l_s, acc_s, att_st, att_all, wo, temporal, wc, ctx_st, ctx_rv,
    codet, wall, wdo, hid, dn, datt, osend,
    load_sem, d2d_send, d2d_recv, kv_send, kv_recv, wo_send, wo_recv, wd_send, wd_recv, att_send, att_recv,
    ctx_send, ctx_recv, out_send, out_recv, self_sem,
):
    s = lax.axis_index("seq")
    t = lax.axis_index("tp")
    y = s // 8
    z = (s // 2) % 4
    c = s % 2
    chip = s // 2
    sib = s + 1 - 2 * c
    tn = (t + 1) % TP
    tb = (t + 3) % TP
    topp = (t + 2) % TP
    half = pl.multiple_of(c * ROWS, ROWS)

    def remote(src, dst, ssem, rsem, seq=None, tp=None):
        return pltpu.make_async_remote_copy(
            src_ref=src, dst_ref=dst, send_sem=ssem, recv_sem=rsem,
            device_id={"seq": s if seq is None else seq, "tp": t if tp is None else tp},
            device_id_type=MESH,
        )

    def cols(ref, start, size):
        return ref.at[:, pl.ds(pl.multiple_of(start * size, size), size)]

    loads = [
        pltpu.make_async_copy(frames_h, frames, load_sem.at[0]),
        pltpu.make_async_copy(wk_h, wqkv.at[:, 0:256], load_sem.at[1]),
        pltpu.make_async_copy(wv_h, wqkv.at[:, 256:512], load_sem.at[2]),
        pltpu.make_async_copy(wq_h, wqkv.at[:, 512:1024], load_sem.at[3]),
        pltpu.make_async_copy(wdq_h, wall.at[t, 0], load_sem.at[4]),
        pltpu.make_async_copy(wdk_h, wall.at[t, 1], load_sem.at[5]),
        pltpu.make_async_copy(wdv_h, wall.at[t, 2], load_sem.at[6]),
        pltpu.make_async_copy(wdo_h, wdo.at[pl.ds(pl.multiple_of(t * 256, 256), 256), :], load_sem.at[7]),
        pltpu.make_async_copy(
            cols(wo_h, t, 512), wo.at[pl.ds(pl.multiple_of(t * 512, 512), 512), :], load_sem.at[8]
        ),
        pltpu.make_async_copy(wc_h, wc, load_sem.at[9]),
        pltpu.make_async_copy(codet_h, codet, load_sem.at[10]),
    ]
    for load in loads:
        load.start()

    barrier = pltpu.get_barrier_semaphore()

    def greet(seq, tp):
        pl.semaphore_signal(barrier, inc=1, device_id={"seq": seq, "tp": tp}, device_id_type=MESH)

    seq_of = (s - 2, s + 2, ((y + 1) % 4) * 8 + s % 8, ((y + 3) % 4) * 8 + s % 8)
    greet(sib, t)
    greet(seq_of[UP], t)
    greet(seq_of[DOWN], t)

    @pl.when(z > 0)
    def _():
        greet(seq_of[LEFT], t)

    @pl.when(z < 3)
    def _():
        greet(seq_of[RIGHT], t)

    for tp in (tn, tb):
        greet(s, tp)
        greet(sib, tp)
    greet(s, topp)

    def greet_source(n, carry):
        src_seq, src_tp = t * 8 + n // TP, n % TP

        @pl.when(jnp.logical_not(jnp.logical_and(src_seq == s, src_tp == t)))
        def _():
            greet(src_seq, src_tp)

        return carry

    lax.fori_loop(0, 32, greet_source, 0)

    loads[0].wait()
    for r in range(4):
        rows = pl.ds(r * 64, 64)
        x = frames[rows, :].astype(F32)
        normed[rows, :] = (x * lax.rsqrt(jnp.mean(x * x, axis=-1, keepdims=True) + 1e-05)).astype(BF16)
    loads[1].wait()
    st[:, 0:256] = dot(normed[...], wqkv[:, 0:256]).astype(BF16)
    loads[2].wait()
    st[:, 256:512] = dot(normed[...], wqkv[:, 256:512]).astype(BF16)

    ends = jnp.where(z > 0, 1, 0) + jnp.where(z < 3, 1, 0)
    own_part = jnp.where(s // 8 == t, 1, 0)
    pl.semaphore_wait(barrier, 3 + ends + 5 + 32 - own_part)

    oc = 1 - c

    def lanes(start, size):
        return pl.ds(pl.multiple_of(start * size, size), size)

    my_rows = pl.ds(half, ROWS)
    d2d = [
        remote(st.at[:, lanes(oc, 128)], kv.at[chip, my_rows, 0:128], d2d_send.at[0], d2d_recv.at[0], seq=sib),
        remote(st.at[:, lanes(2 + oc, 128)], kv.at[chip, my_rows, 128:256], d2d_send.at[1], d2d_recv.at[1], seq=sib),
        remote(st.at[:, lanes(2 + oc, 256)], q_all.at[my_rows, :], d2d_send.at[2], d2d_recv.at[2], seq=sib),
    ]
    d2d[0].start()
    d2d[1].start()
    kv[chip, my_rows, 0:128] = st[:, lanes(c, 128)]
    kv[chip, my_rows, 128:256] = st[:, lanes(2 + c, 128)]

    wo_half = pl.multiple_of(c * 256, 256)

    def wo_rows(tp, core):
        return wo.at[pl.ds(pl.multiple_of(tp * 512 + core * 256, 256), 256), :]

    wo_copies = []
    for n, tp in enumerate((topp, tn, tb)):
        wo_copies.append(
            remote(
                wo_h.at[pl.ds(wo_half, 256), pl.ds(pl.multiple_of(tp * 512, 512), 512)],
                wo_rows(t, c), wo_send.at[n], wo_recv.at[t], tp=tp,
            )
        )
    loads[3].wait()
    st[:, 512:768] = dot(normed[...], wqkv[:, 512:768]).astype(BF16)
    st[:, 768:1024] = dot(normed[...], wqkv[:, 768:1024]).astype(BF16)
    d2d[2].start()
    q_all[my_rows, :] = st[:, lanes(2 + c, 256)]

    def event(e, here):
        if not isinstance(e, int):
            codes = []
            for row in range(4):
                listed = [br * 4 + k for br, k in EVENTS[row]]
                codes.append(pick(e, listed + [-1] * (16 - len(listed))))
            code = jnp.where(y == 0, codes[0], jnp.where(y == 1, codes[1], jnp.where(y == 2, codes[2], codes[3])))
        else:
            code = y * 4
        present = code >= 0
        code = jnp.maximum(code, 0)
        br = code // 4
        k = code % 4
        bz = pick(k, (0, 0, 0, 0))
        for zz in range(4):
            bz = jnp.where(z == zz, pick(k, ORDER[zz]), bz)
        valid = jnp.logical_and(present, jnp.logical_or(br < 3, bz <= z))
        row = br == y
        both = lambda *conds: functools.reduce(jnp.logical_and, conds)
        either = lambda *conds: functools.reduce(jnp.logical_or, conds)
        left = both(valid, row, z > 0, bz >= z, y < 3)
        right = both(valid, row, z < 3, bz <= z)
        up = both(
            valid,
            either(both(row, y < 3), both(y == 1, br == 0, k >= 2), both(y == 2, br == 1, k >= 2)),
        )
        down = both(
            valid,
            either(
                both(row, either(y == 0, both(y == 1, k < 2))),
                both(y == 0, br == 1),
                both(y == 3, br == 0, k < 2),
            ),
        )
        used = both(valid, either(br < y, both(row, bz < z)))
        return br * 4 + bz, valid, used, (left, right, up, down)

    def kv_copy(b, way):
        return remote(kv.at[b], kv.at[b], kv_send.at[way, b], kv_recv.at[b], seq=seq_of[way])

    def forward(b, ways):
        for way in (UP, DOWN, RIGHT, LEFT):
            @pl.when(ways[way])
            def _():
                kv_copy(b, way).start()

    scale = HEAD ** (-0.5) * LOG2E

    def fold(b, first):
        for h in range(2):
            keys = kv[b, :, 0:128]
            values = kv[b, :, 128:256]
            scores = dot_nt(keys, q_all[:, h * 128 : (h + 1) * 128])
            if first:
                kpos = lax.broadcasted_iota(jnp.int32, (PAIR, PAIR), 0)
                qpos = lax.broadcasted_iota(jnp.int32, (PAIR, PAIR), 1)
                scores = jnp.where(kpos <= qpos, scores, NEG)
                top = jnp.max(scores, axis=0, keepdims=True)
                weights = jnp.exp2((scores - top) * scale)
                l_s[h] = jnp.sum(weights, axis=0, keepdims=True)
                acc_s[h] = dot_tn(values, weights.astype(BF16))
                m_s[h] = top
            else:
                old = m_s[h]
                top = jnp.maximum(old, jnp.max(scores, axis=0, keepdims=True))
                weights = jnp.exp2((scores - top) * scale)
                factor = jnp.exp2((old - top) * scale)
                l_s[h] = l_s[h] * factor + jnp.sum(weights, axis=0, keepdims=True)
                acc_s[h] = acc_s[h] * factor + dot_tn(values, weights.astype(BF16))
                m_s[h] = top

    d2d[0].wait_recv()
    d2d[1].wait_recv()
    first_block, _, _, first_ways = event(0, True)
    forward(first_block, first_ways)

    for copy in wo_copies:
        copy.start()

    def qkv_part(tp, lo, n):
        return wall.at[tp, :, pl.ds(pl.multiple_of(lo * 4, 256), n * 4), :]

    def out_part(tp, lo, n):
        return wdo.at[pl.ds(pl.multiple_of(tp * 256 + lo, 64), n), :]

    parts = (qkv_part, out_part)
    mine = c * 128
    theirs = oc * 128

    def wd_direct(p, tp):
        ref = parts[p](t, mine, 128)
        return remote(ref, ref, wd_send.at[p, 0 if tp is tn else 1], wd_recv.at[p, 0 if tp is tn else 1], tp=tp)

    for load in loads[4:8]:
        load.wait()
    for p in range(2):
        for tp in (tn, tb):
            wd_direct(p, tp).start()

    def wd_relay(p, way):
        tp = (tb, tn)[way]
        ref = parts[p](tp, mine + way * 64, 64)
        return remote(ref, ref, wd_send.at[p, 2 + way], wd_recv.at[p, 2 + way], tp=(tn, tb)[way])

    def wd_hand(p, way, core_lo):
        tp = (tb, tn)[way]
        ref = parts[p](tp, core_lo, 128)
        return remote(ref, ref, wd_send.at[p, 4 + way], wd_recv.at[p, 4 + way], seq=sib)

    def wd_hand_relayed(p, way, core_lo):
        ref = parts[p](topp, core_lo + way * 64, 64)
        return remote(ref, ref, wd_send.at[p, 6 + way], wd_recv.at[p, 6 + way], seq=sib)

    def wd_direct_arrived(p, way):
        ref = parts[p]((tb, tn)[way], mine, 128)
        return remote(ref, ref, wd_send.at[p, way], wd_recv.at[p, way], tp=(tn, tb)[way])

    def wd_relay_arrived(p, way):
        ref = parts[p](topp, mine + way * 64, 64)
        return remote(ref, ref, wd_send.at[p, 2 + way], wd_recv.at[p, 2 + way], tp=(tn, tb)[way])

    def wd_pass(p):
        for way in range(2):
            wd_direct_arrived(p, way).wait_recv()
            wd_relay(p, way).start()
            wd_hand(p, way, mine).start()

    def wo_arrived(tp, core, slot):
        ref = wo_rows(tp, core)
        return remote(ref, ref, wo_send.at[0], wo_recv.at[slot], seq=sib)

    d2d[2].wait_recv()
    fold(first_block, True)

    def step(e, carry):
        b, valid, used, ways = event(e, False)

        @pl.when(valid)
        def _():
            kv_copy(b, UP).wait_recv()
            forward(b, ways)

        @pl.when(used)
        def _():
            fold(b, False)

        @pl.when(e == 10)
        def _():
            for n, tp in enumerate((topp, tn, tb)):
                remote(wo_rows(tp, c), wo_rows(tp, c), wo_send.at[n], wo_recv.at[tp], seq=sib).wait_recv()
                remote(wo_rows(tp, c), wo_rows(tp, c), wo_send.at[3 + n], wo_recv.at[4 + tp], seq=sib).start()
            wd_pass(0)

        @pl.when(e == 12)
        def _():
            wd_pass(1)

        return carry

    lax.fori_loop(1, 16, step, 0)

    for h in range(2):
        heads = acc_s[h] / l_s[h]
        heads = heads * lax.rsqrt(jnp.mean(heads * heads, axis=0, keepdims=True) + 1e-06)
        att_st[:, h * 128 : (h + 1) * 128] = heads.T.astype(BF16)

    def att_copy(core, slot, seq, tp):
        return remote(
            att_st.at[pl.ds(pl.multiple_of(core * ROWS, ROWS), ROWS), :], att_all.at[t * 2 + c],
            att_send.at[slot], att_recv.at[t * 2 + c], seq=seq, tp=tp,
        )

    att_copies = [
        att_copy(c, 0, s, tn), att_copy(c, 1, s, tb), att_copy(oc, 2, sib, tn), att_copy(oc, 3, sib, tb),
        att_copy(oc, 4, sib, t),
    ]
    for copy in att_copies:
        copy.start()
    att_all[t * 2 + c] = att_st[my_rows, :]

    loads[10].wait()
    row_level = lax.broadcasted_iota(jnp.int32, (DROWS, LEVELS), 0) % LEVELS
    lane = lax.broadcasted_iota(jnp.int32, (DROWS, LEVELS), 1)
    my_codes = codes_ref[pl.ds(pl.multiple_of(t * QROWS, QROWS), QROWS), :]
    spread = jnp.broadcast_to(my_codes[:, None, :], (QROWS, LEVELS, LEVELS)).reshape(DROWS, LEVELS)
    code = jnp.sum(jnp.where(lane == row_level - 1, spread, 0), axis=-1, keepdims=True)
    level0 = lax.broadcasted_iota(jnp.int32, (DROWS, 1), 0) % LEVELS == 0
    code = jnp.where(level0, -1, code)
    slab_row = lax.broadcasted_iota(jnp.int32, (DROWS, LEVELS), 0) // LEVELS + t * QROWS
    geo = jnp.sum(jnp.where(lane == slab_row, jnp.broadcast_to(geo_ref[...], (DROWS, LEVELS)), 0), axis=-1, keepdims=True)
    code_hot = (lax.broadcasted_iota(jnp.int32, (DROWS, DD), 1) == code).astype(F32).astype(BF16)
    geo_hot = (lax.broadcasted_iota(jnp.int32, (DROWS, 64), 1) == geo).astype(F32).astype(BF16)
    for n in range(4):
        part = slice(n * 256, (n + 1) * 256)
        level = jnp.broadcast_to(level_ref[:, part].astype(F32)[None], (QROWS, LEVELS, 256)).reshape(DROWS, 256)
        hid[:, part] = dot(code_hot, codet[:, part]) + dot(geo_hot, geot_ref[:, part]) + level

    def att_arrived(tp, core):
        ref = att_all.at[tp * 2 + core]
        return remote(ref, ref, att_send.at[0], att_recv.at[tp * 2 + core], seq=sib)

    def att_relay(tp, core, slot, to):
        ref = att_all.at[tp * 2 + core]
        return remote(ref, ref, att_send.at[slot], att_recv.at[tp * 2 + core], tp=to)

    loads[8].wait()
    for n, tp in enumerate((topp, tn, tb)):
        wo_arrived(tp, oc, 4 + tp).wait_recv()

    def project(tp, core):
        rows = pl.ds(pl.multiple_of(tp * 512 + core * 256, 256), 256)
        return dot(att_all[tp * 2 + core], wo[rows, :])

    total = frames[:, pl.ds(pl.multiple_of(t * 512, 512), 512)].astype(F32) + project(t, c)
    att_arrived(t, oc).wait_recv()
    total += project(t, oc)
    relays = [att_relay(tb, 0, 5, tn), att_relay(tn, 1, 6, tb)]
    att_arrived(tb, 0).wait_recv()
    relays[0].start()
    att_arrived(tn, 1).wait_recv()
    relays[1].start()
    total += project(tb, 0) + project(tn, 1)
    for tp, core in ((tb, 1), (tn, 0), (topp, 0), (topp, 1)):
        att_arrived(tp, core).wait_recv()
        total += project(tp, core)
    temporal[...] = total.astype(BF16)
    write = pltpu.make_async_copy(temporal, temporal_h, load_sem.at[11])
    write.start()

    loads[9].wait()
    pick_hot = (lax.broadcasted_iota(jnp.int32, (SEQ, ROWS), 1) == pick_ref[...]).astype(F32).astype(BF16)
    picked = dot(pick_hot, temporal[...]).astype(BF16)
    for n in range(8):
        ctx_st[:, n, :] = dot(picked, wc[:, n * 128 : (n + 1) * 128])
    to_tp = s // 8
    slot = (s % 8) * TP + t

    def ctx_copy(j):
        return remote(
            ctx_st.at[j], ctx_rv.at[slot], ctx_send.at[j], ctx_recv.at[slot], seq=j, tp=to_tp
        )

    own_ctx = pltpu.make_async_copy(ctx_st.at[s], ctx_rv.at[slot], self_sem)
    stays = to_tp == t

    def ctx_out(j, carry):
        @pl.when(jnp.logical_not(jnp.logical_and(j == s, stays)))
        def _():
            ctx_copy(j).start()

        return carry

    lax.fori_loop(0, SEQ, ctx_out, 0)

    @pl.when(stays)
    def _():
        own_ctx.start()
        own_ctx.wait()

    for p in range(2):
        for way in range(2):
            wd_relay_arrived(p, way).wait_recv()
            wd_hand_relayed(p, way, mine).start()

    def ctx_in(n, carry):
        @pl.when(jnp.logical_not(jnp.logical_and(n == slot, stays)))
        def _():
            ref = ctx_rv.at[n]
            remote(ref, ref, ctx_send.at[n], ctx_recv.at[n], seq=sib).wait_recv()

        return carry

    lax.fori_loop(0, SEQ, ctx_in, 0)

    square = jnp.zeros((DROWS, 1), F32)
    for n in range(8):
        part = slice(n * 128, (n + 1) * 128)
        rows = []
        for r in range(QROWS):
            row = ctx_rv[r * TP, n : n + 1, :]
            for tp in range(1, TP):
                row = row + ctx_rv[r * TP + tp, n : n + 1, :]
            rows.append(jnp.broadcast_to(row.astype(BF16).astype(F32), (LEVELS, 128)))
        value = hid[:, part] + jnp.concatenate(rows, axis=0)
        hid[:, part] = value
        square += jnp.sum(value * value, axis=-1, keepdims=True)
    factor = lax.rsqrt(square * (1.0 / DD) + 1e-05)
    dn[...] = (hid[...] * factor).astype(BF16)

    for p in range(2):
        for way in range(2):
            wd_hand(p, way, theirs).wait_recv()
            wd_hand_relayed(p, way, theirs).wait_recv()

    dscale = DHEAD ** (-0.5) * LOG2E
    lrow = lax.broadcasted_iota(jnp.int32, (128, 128), 0)
    lcol = lax.broadcasted_iota(jnp.int32, (128, 128), 1)
    allowed = jnp.logical_and(lrow // LEVELS == lcol // LEVELS, lcol <= lrow)

    def depth_heads(g, carry):
        queries = dot(dn[...], wall[g, 0]).astype(BF16)
        keys = dot(dn[...], wall[g, 1]).astype(BF16)
        values = dot(dn[...], wall[g, 2]).astype(BF16)
        outs = []
        for r in range(2):
            rows = slice(r * 128, (r + 1) * 128)
            parts_out = []
            for h in range(4):
                part = slice(h * DHEAD, (h + 1) * DHEAD)
                scores = dot_nt(queries[rows, part], keys[rows, part])
                scores = jnp.where(allowed, scores, NEG)
                top = jnp.max(scores, axis=-1, keepdims=True)
                weights = jnp.exp2((scores - top) * dscale)
                sums = jnp.sum(weights, axis=-1, keepdims=True)
                heads = dot(weights.astype(BF16), values[rows, part]) / sums
                heads = heads * lax.rsqrt(jnp.mean(heads * heads, axis=-1, keepdims=True) + 1e-06)
                parts_out.append(heads.astype(BF16))
            outs.append(jnp.concatenate(parts_out, axis=1))
        datt[:, pl.ds(pl.multiple_of(g * 256, 256), 256)] = jnp.concatenate(outs, axis=0)
        return carry

    lax.fori_loop(0, TP, depth_heads, 0)

    def out_tile(tp):
        part = pl.ds(pl.multiple_of(tp * 256, 256), 256)
        return (dot(datt[...], wdo[:, part]) + hid[:, part]).astype(BF16)

    def out_rows(tp):
        return depth_h.at[pl.ds(pl.multiple_of(tp * DROWS, DROWS), DROWS), :]

    out_copies = []
    for n, tp in enumerate((topp, tn, tb)):
        osend[n] = out_tile(tp)
        copy = remote(osend.at[n], out_rows(t), out_send.at[n], out_recv.at[t], tp=tp)
        copy.start()
        out_copies.append(copy)
    osend[3] = out_tile(t)
    own_out = pltpu.make_async_copy(osend.at[3], out_rows(t), load_sem.at[12])
    own_out.start()

    for copy in d2d + wo_copies + att_copies + relays:
        copy.wait_send()
    for n, tp in enumerate((topp, tn, tb)):
        remote(wo_rows(tp, c), wo_rows(tp, c), wo_send.at[3 + n], wo_recv.at[4 + tp], seq=sib).wait_send()
    for p in range(2):
        for tp in (tn, tb):
            wd_direct(p, tp).wait_send()
        for way in range(2):
            wd_relay(p, way).wait_send()
            wd_hand(p, way, mine).wait_send()
            wd_hand_relayed(p, way, mine).wait_send()

    def sent(e, carry):
        b, _, _, ways = event(e, False)
        for way in range(4):
            @pl.when(ways[way])
            def _():
                kv_copy(b, way).wait_send()

        return carry

    for way in range(4):
        @pl.when(first_ways[way])
        def _():
            kv_copy(first_block, way).wait_send()

    lax.fori_loop(1, 16, sent, 0)

    def ctx_sent(j, carry):
        @pl.when(jnp.logical_not(jnp.logical_and(j == s, stays)))
        def _():
            ctx_copy(j).wait_send()

        return carry

    lax.fori_loop(0, SEQ, ctx_sent, 0)
    write.wait()
    own_out.wait()
    for n, tp in enumerate((topp, tn, tb)):
        out_copies[n].wait_send()
    for tp in (topp, tn, tb):
        remote(osend.at[0], out_rows(tp), out_send.at[0], out_recv.at[tp], tp=tp).wait_recv()


def body(
    frames, w_query, w_key, w_value, w_out, frame_pick, codes, geo_ids, geo_table, w_context, code_table,
    level_table, wd_query, wd_key, wd_value, wd_out,
):
    hbm = pl.BlockSpec(memory_space=pl.ANY)
    vmem = pl.BlockSpec(memory_space=pltpu.VMEM)
    sem = pltpu.SemaphoreType.DMA
    temporal, depth = pl.pallas_call(
        kernel,
        out_shape=(
            jax.ShapeDtypeStruct((ROWS, 512), BF16),
            jax.ShapeDtypeStruct((SEQ * LEVELS, 256), BF16),
        ),
        in_specs=[hbm, hbm, hbm, hbm, hbm, vmem, vmem, vmem, vmem, hbm, hbm, vmem, hbm, hbm, hbm, hbm],
        out_specs=(hbm, hbm),
        scratch_shapes=[
            pltpu.VMEM((ROWS, D), BF16),
            pltpu.VMEM((ROWS, D), BF16),
            pltpu.VMEM((D, 1024), BF16),
            pltpu.VMEM((ROWS, 1024), BF16),
            pltpu.VMEM((PAIR, 256), BF16),
            pltpu.VMEM((CHIPS, PAIR, 256), BF16),
            pltpu.VMEM((2, 1, PAIR), F32),
            pltpu.VMEM((2, 1, PAIR), F32),
            pltpu.VMEM((2, HEAD, PAIR), F32),
            pltpu.VMEM((PAIR, 256), BF16),
            pltpu.VMEM((TP * 2, ROWS, 256), BF16),
            pltpu.VMEM((D, 512), BF16),
            pltpu.VMEM((ROWS, 512), BF16),
            pltpu.VMEM((512, DD), BF16),
            pltpu.VMEM((SEQ, 8, 128), F32),
            pltpu.VMEM((SEQ, 8, 128), F32),
            pltpu.VMEM((DD, DD), BF16),
            pltpu.VMEM((TP, 3, DD, 256), BF16),
            pltpu.VMEM((DD, DD), BF16),
            pltpu.VMEM((DROWS, DD), F32),
            pltpu.VMEM((DROWS, DD), BF16),
            pltpu.VMEM((DROWS, DD), BF16),
            pltpu.VMEM((TP, DROWS, 256), BF16),
            sem((13,)),
            sem((3,)),
            sem((3,)),
            sem((4, CHIPS)),
            sem((CHIPS,)),
            sem((6,)),
            sem((8,)),
            sem((2, 8)),
            sem((2, 8)),
            sem((7,)),
            sem((8,)),
            sem((SEQ,)),
            sem((SEQ,)),
            sem((3,)),
            sem((TP,)),
            sem(()),
        ],
        compiler_params=pltpu.CompilerParams(
            collective_id=0, has_side_effects=True, vmem_limit_bytes=58 * 1024 * 1024
        ),
        name="codec_layers",
    )(
        frames, w_query, w_key, w_value, w_out, frame_pick.reshape(SEQ, 1), codes, geo_ids.reshape(1, SEQ),
        geo_table, w_context, code_table, level_table, wd_query, wd_key, wd_value, wd_out,
    )
    return temporal, depth.reshape(SEQ, LEVELS, 256)


def solution(mesh):
    return jax.shard_map(
        body,
        mesh=mesh,
        in_specs=(
            P(("dp", "seq"), None),
            P(None, "tp"),
            P(None, "tp"),
            P(None, "tp"),
            P("tp", None),
            P(("dp", "seq"), None, None),
            P(("dp", "seq"), None),
            P(("dp", "seq")),
            P(),
            P("tp", None),
            P(),
            P(),
            P(None, "tp"),
            P(None, "tp"),
            P(None, "tp"),
            P("tp", None),
        ),
        out_specs=(P(("dp", "seq"), "tp"), P(("dp", "seq"), None, "tp")),
        check_vma=False,
    )
```

```python
import functools
import math

import jax
import jax.numpy as jnp
from jax import lax
from jax.experimental import pallas as pl
from jax.experimental.pallas import tpu as pltpu
from jax.sharding import PartitionSpec as P

MESH = pl.DeviceIdType.MESH
BF16 = jnp.bfloat16
F32 = jnp.float32
LOG2E = math.log2(math.e)

ROWS = 256
D = 2048
HEAD = 128
DD = 1024
DHEAD = 64
LEVELS = 32
SEQ = 32
TP = 4
CHIPS = 16
PAIR = 2 * ROWS
QROWS = 8
DROWS = QROWS * LEVELS
NEG = -1e30

EVENTS = (
    ((0, 0), (0, 1), (1, 0), (1, 1), (0, 2), (0, 3)),
    ((1, 0), (1, 1), (0, 0), (0, 1), (1, 2), (0, 2), (1, 3), (0, 3)),
    ((2, 0), (2, 1), (1, 0), (0, 0), (1, 1), (0, 1), (2, 2), (1, 2), (0, 2), (2, 3), (1, 3), (0, 3)),
    (
        (3, 0), (3, 1), (2, 0), (0, 0), (2, 1), (0, 1), (1, 0), (3, 2),
        (2, 2), (1, 1), (1, 2), (0, 2), (3, 3), (2, 3), (0, 3), (1, 3),
    ),
)
ORDER = tuple(tuple(z ^ k for k in range(4)) for z in range(4))
ACROSS, UP, DOWN = range(3)


def event_fields(y, z, e):
    if e >= len(EVENTS[y]):
        return 0
    br, k = EVENTS[y][e]
    bz = ORDER[z][k]
    if br == 3 and bz // 2 > z // 2:
        return 0
    row = br == y
    across = row and k < 2 and (y < 3 or z < 2)
    up = (row and y < 3) or (y == 1 and br == 0 and k >= 2) or (y == 2 and br == 1 and k >= 2)
    down = (row and (y == 0 or (y == 1 and k < 2))) or (y == 0 and br == 1) or (y == 3 and br == 0 and k < 2)
    used = br < y or (row and bz // 2 <= z // 2)
    bits = br * 4 + bz
    for place, flag in enumerate((True, used, across, up, down)):
        bits += int(flag) << (4 + place)
    return bits


EVENT_WORDS = tuple(
    tuple(
        sum(event_fields(n // 4, n % 4, 3 * w + i) << (10 * i) for i in range(3)) for n in range(CHIPS)
    )
    for w in range(6)
)


def pick(index, values):
    out = jnp.int32(values[0]) if isinstance(values[0], int) else values[0]
    for place, value in enumerate(values[1:], 1):
        out = jnp.where(index == place, jnp.int32(value) if isinstance(value, int) else value, out)
    return out


def dot(a, b):
    return jnp.dot(a, b, preferred_element_type=F32)


def dot_nt(a, b):
    return lax.dot_general(a, b, (((1,), (1,)), ((), ())), preferred_element_type=F32)


def dot_tn(a, b):
    return lax.dot_general(a, b, (((0,), (0,)), ((), ())), preferred_element_type=F32)


def kernel(
    frames_h, wq_h, wk_h, wv_h, wo_h, pick_ref, codes_ref, geo_ref, geot_ref, wc_h, codet_h, level_ref,
    wdq_h, wdk_h, wdv_h, wdo_h,
    temporal_h, depth_h,
    frames, normed, wqkv, kv_st, q_st, q_all, kv, m_s, l_s, acc_s, att_st, att_all, wo, temporal, wc, ctx_st, ctx_in, ctx_mine, ctx_rv,
    codet, wall, wdo, hid, dn, datt, osend,
    load_sem, d2d_send, q_recv, kv_send, kv_recv, sib_send, sib_recv, wo_send, wo_recv, wd_send, wd_recv, att_send, att_recv,
    ctx_send, ctx_recv, row_send, row_recv, out_send, out_recv, self_sem,
):
    s = lax.axis_index("seq")
    t = lax.axis_index("tp")
    y = s // 8
    z = (s // 2) % 4
    c = s % 2
    chip = s // 2
    sib = s + 1 - 2 * c
    tn = (t + 1) % TP
    tb = (t + 3) % TP
    topp = (t + 2) % TP
    half = pl.multiple_of(c * ROWS, ROWS)

    def remote(src, dst, ssem, rsem, seq=None, tp=None):
        return pltpu.make_async_remote_copy(
            src_ref=src, dst_ref=dst, send_sem=ssem, recv_sem=rsem,
            device_id={"seq": s if seq is None else seq, "tp": t if tp is None else tp},
            device_id_type=MESH,
        )

    def cols(ref, start, size):
        return ref.at[:, pl.ds(pl.multiple_of(start * size, size), size)]

    loads = [
        pltpu.make_async_copy(frames_h, frames, load_sem.at[0]),
        pltpu.make_async_copy(wk_h, wqkv.at[:, 0:256], load_sem.at[1]),
        pltpu.make_async_copy(wv_h, wqkv.at[:, 256:512], load_sem.at[2]),
        pltpu.make_async_copy(wq_h, wqkv.at[:, 512:1024], load_sem.at[3]),
        pltpu.make_async_copy(wdq_h, wall.at[t, 0], load_sem.at[4]),
        pltpu.make_async_copy(wdk_h, wall.at[t, 1], load_sem.at[5]),
        pltpu.make_async_copy(wdv_h, wall.at[t, 2], load_sem.at[6]),
        pltpu.make_async_copy(wdo_h, wdo.at[pl.ds(pl.multiple_of(t * 256, 256), 256), :], load_sem.at[7]),
        pltpu.make_async_copy(
            cols(wo_h, t, 512), wo.at[pl.ds(pl.multiple_of(t * 512, 512), 512), :], load_sem.at[8]
        ),
        pltpu.make_async_copy(wc_h, wc, load_sem.at[9]),
        pltpu.make_async_copy(codet_h, codet, load_sem.at[10]),
    ]
    for load in loads:
        load.start()

    barrier = pltpu.get_barrier_semaphore()

    def greet(seq, tp):
        pl.semaphore_signal(barrier, inc=1, device_id={"seq": seq, "tp": tp}, device_id_type=MESH)

    p = z % 2
    op = 1 - p
    mate = s + 2 * (1 - 2 * p)
    mate_sib = sib + 2 * (1 - 2 * p)
    seq_of = (s + 4 * (1 - 2 * (z // 2)), ((y + 1) % 4) * 8 + s % 8, ((y + 3) % 4) * 8 + s % 8)
    greet(sib, t)
    greet(mate, t)
    greet(mate_sib, t)
    for way in range(3):
        greet(seq_of[way], t)
    for tp in (tn, tb):
        greet(s, tp)
        greet(sib, tp)
    greet(s, topp)

    for n in range(QROWS):
        @pl.when(jnp.logical_not(jnp.logical_and(t * 8 + n == s, s // 8 == t)))
        def _():
            greet(t * 8 + n, s // 8)

    loads[0].wait()
    for r in range(4):
        rows = pl.ds(r * 64, 64)
        x = frames[rows, :].astype(F32)
        normed[rows, :] = (x * lax.rsqrt(jnp.mean(x * x, axis=-1, keepdims=True) + 1e-05)).astype(BF16)
    loads[1].wait()
    both = dot(normed[...], wqkv[:, 0:256]).astype(BF16)
    kv_st[0, :, 0:128] = both[:, 0:128]
    kv_st[1, :, 0:128] = both[:, 128:256]
    loads[2].wait()
    both = dot(normed[...], wqkv[:, 256:512]).astype(BF16)
    kv_st[0, :, 128:256] = both[:, 0:128]
    kv_st[1, :, 128:256] = both[:, 128:256]

    own_part = jnp.where(s // 8 == t, 1, 0)
    pl.semaphore_wait(barrier, 6 + 5 + QROWS - own_part)

    oc = 1 - c
    my_rows = pl.ds(half, ROWS)
    other_rows = pl.ds(pl.multiple_of(oc * ROWS, ROWS), ROWS)

    def kv_half(b, rows):
        return kv.at[b, rows, :]

    kv_mate = remote(kv_st.at[op], kv_half(chip, my_rows), d2d_send.at[0], kv_recv.at[chip], seq=mate)
    kv_sib = remote(kv_st.at[p], kv_half(chip, my_rows), d2d_send.at[1], sib_recv.at[chip], seq=sib)
    kv_mate.start()
    kv_sib.start()
    kv[chip, my_rows, :] = kv_st[p]

    def kv_copy(b, way):
        return remote(kv_half(b, my_rows), kv_half(b, my_rows), kv_send.at[way, b], kv_recv.at[b], seq=seq_of[way])

    def sib_copy(b):
        return remote(kv_half(b, my_rows), kv_half(b, my_rows), sib_send.at[b], sib_recv.at[b], seq=sib)

    def forward(b, ways):
        for way in (DOWN, UP, ACROSS):
            @pl.when(ways[way])
            def _():
                kv_copy(b, way).start()

    words = [pick(chip, table) for table in EVENT_WORDS]

    def event(e):
        word = pick(e // 3, words)
        place = e % 3
        bits = jnp.where(place == 0, word, jnp.where(place == 1, word // 1024, word // (1024 * 1024)))
        flags = [(bits // (16 << n)) % 2 == 1 for n in range(5)]
        return bits % 16, flags[0], flags[1], flags[2:]

    first_block, _, _, first_ways = event(jnp.int32(0))
    forward(first_block, first_ways)

    q_slot = p * 2 + c

    def q_copy(n, seq, head):
        return remote(q_st.at[head], q_all.at[q_slot], d2d_send.at[2 + n], q_recv.at[q_slot], seq=seq)

    q_copies = [
        q_copy(0, mate, op * 2 + c), q_copy(1, mate_sib, op * 2 + oc), q_copy(2, sib, p * 2 + oc),
    ]

    wo_half = pl.multiple_of(c * 256, 256)

    def wo_rows(tp, core):
        return wo.at[pl.ds(pl.multiple_of(tp * 512 + core * 256, 256), 256), :]

    wo_copies = []
    for n, tp in enumerate((topp, tn, tb)):
        wo_copies.append(
            remote(
                wo_h.at[pl.ds(wo_half, 256), pl.ds(pl.multiple_of(tp * 512, 512), 512)],
                wo_rows(t, c), wo_send.at[n], wo_recv.at[t], tp=tp,
            )
        )
    def wo_sends():
        for copy in wo_copies:
            copy.start()

    def square_part(m):
        def part(tp, lo, n):
            return wall.at[tp, m, pl.ds(pl.multiple_of(lo * 4, 256), n * 4), :]

        return part

    def out_part(tp, lo, n):
        return wdo.at[pl.ds(pl.multiple_of(tp * 256 + lo, 64), n), :]

    parts = (square_part(0), square_part(1), square_part(2), out_part)
    PARTS = len(parts)
    mine = c * 128
    theirs = oc * 128

    def wd_direct(p, way):
        if p < 3:
            src = (wdq_h, wdk_h, wdv_h)[p].at[pl.ds(pl.multiple_of(mine * 4, 512), 512), :]
        else:
            src = wdo_h.at[pl.ds(pl.multiple_of(mine, 128), 128), :]
        return remote(src, parts[p](t, mine, 128), wd_send.at[p, way], wd_recv.at[p, way], tp=(tn, tb)[way])

    def wd_start(p):
        for way in range(2):
            wd_direct(p, way).start()

    def wd_first():
        wd_start(0)
        wd_start(1)

    def wd_relay(p, way):
        tp = (tb, tn)[way]
        ref = parts[p](tp, mine + way * 64, 64)
        return remote(ref, ref, wd_send.at[p, 2 + way], wd_recv.at[p, 2 + way], tp=(tn, tb)[way])

    def wd_hand(p, way, core_lo):
        tp = (tb, tn)[way]
        ref = parts[p](tp, core_lo, 128)
        return remote(ref, ref, wd_send.at[p, 4 + way], wd_recv.at[p, 4 + way], seq=sib)

    def wd_hand_relayed(p, way, core_lo):
        ref = parts[p](topp, core_lo + way * 64, 64)
        return remote(ref, ref, wd_send.at[p, 6 + way], wd_recv.at[p, 6 + way], seq=sib)

    def wd_direct_arrived(p, way):
        ref = parts[p]((tb, tn)[way], mine, 128)
        return remote(ref, ref, wd_send.at[p, way], wd_recv.at[p, way], tp=(tn, tb)[way])

    def wd_relay_arrived(p, way):
        ref = parts[p](topp, mine + way * 64, 64)
        return remote(ref, ref, wd_send.at[p, 2 + way], wd_recv.at[p, 2 + way], tp=(tn, tb)[way])

    def wd_pass(p):
        for way in range(2):
            wd_direct_arrived(p, way).wait_recv()
            wd_relay(p, way).start()
            wd_hand(p, way, mine).start()

    def wo_arrived(tp, core, slot):
        ref = wo_rows(tp, core)
        return remote(ref, ref, wo_send.at[0], wo_recv.at[slot], seq=sib)

    wo_sends()
    wd_first()
    loads[3].wait()
    scale = HEAD ** (-0.5) * LOG2E
    for n in range(2):
        both = (dot(normed[...], wqkv[:, 512 + n * 256 : 768 + n * 256]) * scale).astype(BF16)
        q_st[2 * n] = both[:, 0:128]
        q_st[2 * n + 1] = both[:, 128:256]
    for copy in q_copies:
        copy.start()
    q_all[q_slot] = q_st[q_slot]


    for h in range(2):
        m_s[h] = jnp.full((1, PAIR), NEG, F32)
        l_s[h] = jnp.zeros((1, PAIR), F32)
        acc_s[h] = jnp.zeros((HEAD, PAIR), F32)

    def fold(b, masked):
        for h in range(2):
            keys = kv[b, :, 0:128]
            values = kv[b, :, 128:256]
            queries = q_all[2 * h : 2 * h + 2].reshape(PAIR, HEAD)
            scores = dot_nt(keys, queries)
            if masked:
                ahead = (b - (chip // 2 * 2 + h)) * PAIR
                kpos = lax.broadcasted_iota(jnp.int32, (PAIR, PAIR), 0) + ahead
                qpos = lax.broadcasted_iota(jnp.int32, (PAIR, PAIR), 1)
                scores = jnp.where(kpos <= qpos, scores, NEG)
            old = m_s[h]
            top = jnp.maximum(old, jnp.max(scores, axis=0, keepdims=True))
            weights = jnp.exp2(scores - top)
            factor = jnp.exp2(old - top)
            l_s[h] = l_s[h] * factor + jnp.sum(weights, axis=0, keepdims=True)
            acc_s[h] = acc_s[h] * factor + dot_tn(values, weights.astype(BF16))
            m_s[h] = top

    def fold_arrived(b, used):
        @pl.when(used)
        def _():
            remote(
                kv_half(b, other_rows), kv_half(b, other_rows), sib_send.at[b], sib_recv.at[b], seq=sib
            ).wait_recv()

        masked = b // 2 == chip // 2

        @pl.when(jnp.logical_and(used, masked))
        def _():
            fold(b, True)

        @pl.when(jnp.logical_and(used, jnp.logical_not(masked)))
        def _():
            fold(b, False)

    for head in range(4):
        @pl.when(head != q_slot)
        def _():
            remote(q_all.at[head], q_all.at[head], d2d_send.at[0], q_recv.at[head], seq=sib).wait_recv()

    def step(e, before):
        b, valid, used, ways = event(e)

        @pl.when(valid)
        def _():
            kv_copy(b, UP).wait_recv()
            forward(b, ways)

        @pl.when(used)
        def _():
            sib_copy(b).start()

        fold_arrived(before[0], before[1] > 0)

        @pl.when(e == 5)
        def _():
            wd_pass(0)
            wd_start(2)

        @pl.when(e == 9)
        def _():
            wd_pass(1)
            wd_start(3)

        @pl.when(e == 12)
        def _():
            for n, tp in enumerate((topp, tn, tb)):
                remote(wo_rows(tp, c), wo_rows(tp, c), wo_send.at[n], wo_recv.at[tp], seq=sib).wait_recv()
                remote(wo_rows(tp, c), wo_rows(tp, c), wo_send.at[3 + n], wo_recv.at[4 + tp], seq=sib).start()

        return b, used.astype(jnp.int32)

    last = lax.fori_loop(1, 16, step, (first_block, jnp.int32(1)))
    fold_arrived(last[0], last[1] > 0)

    my_lanes = pl.ds(pl.multiple_of(q_slot * HEAD, HEAD), HEAD)

    def att_at(tp, head):
        return att_all.at[tp, :, pl.ds(pl.multiple_of(head * HEAD, HEAD), HEAD)]

    def att_copy(n, group, seq, tp):
        return remote(
            att_st.at[group], att_at(t, q_slot), att_send.at[n], att_recv.at[t, q_slot], seq=seq, tp=tp
        )

    att_copies = [
        att_copy(0, op * 2 + c, mate, t), att_copy(1, op * 2 + oc, mate_sib, t),
        att_copy(2, p * 2 + c, s, tn), att_copy(3, p * 2 + c, s, tb),
        att_copy(4, p * 2 + oc, sib, tn), att_copy(5, p * 2 + oc, sib, tb), att_copy(6, p * 2 + oc, sib, t),
    ]
    for h in range(2):
        heads = acc_s[h] / l_s[h]
        heads = heads * lax.rsqrt(jnp.mean(heads * heads, axis=0, keepdims=True) + 1e-06)
        heads = heads.T.astype(BF16)
        att_st[2 * h] = heads[0:256]
        att_st[2 * h + 1] = heads[256:512]
    for copy in att_copies:
        copy.start()
    att_all[t, :, my_lanes] = att_st[q_slot]

    def att_pass(n, tp, head, to):
        return remote(att_at(tp, head), att_at(tp, head), att_send.at[n], att_recv.at[tp, head], tp=to)

    def att_arrived(tp, head):
        att_pass(0, tp, head, tn).wait_recv()

    mate_copies = []
    for core in range(2):
        for way, to in enumerate((tn, tb)):
            mate_copies.append(att_pass(7 + 2 * core + way, t, op * 2 + core, to))
    for core in range(2):
        att_arrived(t, op * 2 + core)
        mate_copies[2 * core].start()
        mate_copies[2 * core + 1].start()

    loads[10].wait()
    row_level = lax.broadcasted_iota(jnp.int32, (DROWS, LEVELS), 0) % LEVELS
    lane = lax.broadcasted_iota(jnp.int32, (DROWS, LEVELS), 1)
    my_codes = codes_ref[pl.ds(pl.multiple_of(t * QROWS, QROWS), QROWS), :]
    spread = jnp.broadcast_to(my_codes[:, None, :], (QROWS, LEVELS, LEVELS)).reshape(DROWS, LEVELS)
    code = jnp.sum(jnp.where(lane == row_level - 1, spread, 0), axis=-1, keepdims=True)
    level0 = lax.broadcasted_iota(jnp.int32, (DROWS, 1), 0) % LEVELS == 0
    code = jnp.where(level0, -1, code)
    slab_row = lax.broadcasted_iota(jnp.int32, (DROWS, LEVELS), 0) // LEVELS + t * QROWS
    geo = jnp.sum(jnp.where(lane == slab_row, jnp.broadcast_to(geo_ref[...], (DROWS, LEVELS)), 0), axis=-1, keepdims=True)
    code_hot = (lax.broadcasted_iota(jnp.int32, (DROWS, DD), 1) == code).astype(F32).astype(BF16)
    geo_hot = (lax.broadcasted_iota(jnp.int32, (DROWS, 64), 1) == geo).astype(F32).astype(BF16)
    for n in range(4):
        part = slice(n * 256, (n + 1) * 256)
        level = jnp.broadcast_to(level_ref[:, part].astype(F32)[None], (QROWS, LEVELS, 256)).reshape(DROWS, 256)
        hid[:, part] = dot(code_hot, codet[:, part]) + dot(geo_hot, geot_ref[:, part]) + level

    loads[8].wait()
    for n, tp in enumerate((topp, tn, tb)):
        wo_arrived(tp, oc, 4 + tp).wait_recv()

    def project(tp):
        rows = pl.ds(pl.multiple_of(tp * 512, 512), 512)
        return dot(att_all[tp], wo[rows, :])

    att_arrived(t, p * 2 + oc)
    total = frames[:, pl.ds(pl.multiple_of(t * 512, 512), 512)].astype(F32) + project(t)
    relays = []
    for core, head_of in ((0, p * 2), (1, op * 2)):
        for tp, to, odd in ((tb, tn, 0), (tn, tb, 1)):
            relays.append(att_pass(11 + len(relays), tp, head_of + odd, to))
            att_arrived(tp, head_of + odd)
            relays[-1].start()
    for tp, odd in ((tb, 1), (tn, 0)):
        att_arrived(tp, odd)
        att_arrived(tp, 2 + odd)
        total += project(tp)
    for head in range(4):
        att_arrived(topp, head)
    total += project(topp)
    temporal[...] = total.astype(BF16)
    write = pltpu.make_async_copy(temporal, temporal_h, load_sem.at[11])
    write.start()

    wd_pass(2)

    loads[9].wait()
    pick_hot = (lax.broadcasted_iota(jnp.int32, (ROWS, SEQ), 0) == pick_ref[...]).astype(F32).astype(BF16)
    picked = dot_tn(pick_hot, temporal[...]).astype(BF16)
    for n in range(8):
        ctx_st[:, n, :] = dot(picked, wc[:, n * 128 : (n + 1) * 128])
    def ctx_rows(u):
        return ctx_st.at[pl.ds(pl.multiple_of(u * QROWS, QROWS), QROWS)]

    def ctx_copy(n, tp):
        return remote(ctx_rows(tp), ctx_in.at[t], ctx_send.at[n], ctx_recv.at[t], tp=tp)

    ctx_copies = [ctx_copy(n, tp) for n, tp in enumerate((topp, tn, tb))]
    for copy in ctx_copies:
        copy.start()

    wd_pass(3)

    ctx_total = ctx_st[pl.ds(pl.multiple_of(t * QROWS, QROWS), QROWS)].astype(BF16).astype(F32)
    for tp in (tn, tb, topp):
        remote(ctx_in.at[tp], ctx_in.at[tp], ctx_send.at[0], ctx_recv.at[tp], tp=tp).wait_recv()
        ctx_total = ctx_total + ctx_in[tp].astype(BF16).astype(F32)
    ctx_mine[...] = ctx_total.astype(BF16).astype(F32)

    to_tp = s // 8
    stays = to_tp == t
    place = s % 8

    def row_copy(n):
        return remote(ctx_mine.at[n], ctx_rv.at[place], row_send.at[n], row_recv.at[place], seq=t * 8 + n, tp=to_tp)

    def is_self(n):
        return jnp.logical_and(t * 8 + n == s, stays)

    for n in range(QROWS):
        @pl.when(jnp.logical_not(is_self(n)))
        def _():
            row_copy(n).start()

    own_row = pltpu.make_async_copy(ctx_mine.at[place], ctx_rv.at[place], self_sem)

    @pl.when(stays)
    def _():
        own_row.start()
        own_row.wait()

    for n in range(QROWS):
        @pl.when(jnp.logical_not(is_self(n)))
        def _():
            ref = ctx_rv.at[n]
            remote(ref, ref, row_send.at[n], row_recv.at[n], seq=sib).wait_recv()

    for load in loads[4:8]:
        load.wait()

    square = jnp.zeros((DROWS, 1), F32)
    for n in range(8):
        part = slice(n * 128, (n + 1) * 128)
        rows = []
        for r in range(QROWS):
            rows.append(jnp.broadcast_to(ctx_rv[r, n : n + 1, :], (LEVELS, 128)))
        value = hid[:, part] + jnp.concatenate(rows, axis=0)
        hid[:, part] = value
        square += jnp.sum(value * value, axis=-1, keepdims=True)
    factor = lax.rsqrt(square * (1.0 / DD) + 1e-05)
    dn[...] = (hid[...] * factor).astype(BF16)

    dscale = DHEAD ** (-0.5) * LOG2E
    lrow = lax.broadcasted_iota(jnp.int32, (128, 128), 0)
    lcol = lax.broadcasted_iota(jnp.int32, (128, 128), 1)
    allowed = jnp.logical_and(lrow // LEVELS == lcol // LEVELS, lrow <= lcol)

    for n, g in enumerate((t, tb, tn, topp)):
        if n == 1 or n == 2:
            for p in range(3):
                wd_hand(p, n - 1, theirs).wait_recv()
        if n == 2:
            for p in range(PARTS):
                for way in range(2):
                    wd_relay_arrived(p, way).wait_recv()
                    wd_hand_relayed(p, way, mine).start()
        if n == 3:
            for p in range(3):
                for way in range(2):
                    wd_hand_relayed(p, way, theirs).wait_recv()
        queries = (dot(dn[...], wall[g, 0]) * dscale).astype(BF16)
        keys = dot(dn[...], wall[g, 1]).astype(BF16)
        values = dot(dn[...], wall[g, 2]).astype(BF16)
        for r in range(2):
            rows = slice(r * 128, (r + 1) * 128)
            outs = []
            for h in range(4):
                part = slice(h * DHEAD, (h + 1) * DHEAD)
                scores = dot_nt(keys[rows, part], queries[rows, part])
                scores = jnp.where(allowed, scores, NEG)
                top = jnp.max(scores, axis=0, keepdims=True)
                weights = jnp.exp2(scores - top)
                sums = jnp.sum(weights, axis=0, keepdims=True)
                heads = dot_tn(values[rows, part], weights.astype(BF16)) / sums
                heads = heads * lax.rsqrt(jnp.mean(heads * heads, axis=0, keepdims=True) + 1e-06)
                outs.append(heads)
            datt[rows, pl.ds(pl.multiple_of(g * 256, 256), 256)] = jnp.concatenate(outs, axis=0).T.astype(BF16)

    for way in range(2):
        wd_hand(3, way, theirs).wait_recv()
        wd_hand_relayed(3, way, theirs).wait_recv()

    def out_tile(tp):
        part = pl.ds(pl.multiple_of(tp * 256, 256), 256)
        return (dot(datt[...], wdo[:, part]) + hid[:, part]).astype(BF16)

    def out_rows(tp):
        return depth_h.at[pl.ds(pl.multiple_of(tp * DROWS, DROWS), DROWS), :]

    out_copies = []
    for n, tp in enumerate((topp, tn, tb)):
        osend[n] = out_tile(tp)
        copy = remote(osend.at[n], out_rows(t), out_send.at[n], out_recv.at[t], tp=tp)
        copy.start()
        out_copies.append(copy)
    osend[3] = out_tile(t)
    own_out = pltpu.make_async_copy(osend.at[3], out_rows(t), load_sem.at[12])
    own_out.start()

    for copy in [kv_mate, kv_sib] + q_copies + wo_copies + att_copies + mate_copies + relays:
        copy.wait_send()
    for n, tp in enumerate((topp, tn, tb)):
        remote(wo_rows(tp, c), wo_rows(tp, c), wo_send.at[3 + n], wo_recv.at[4 + tp], seq=sib).wait_send()
    for p in range(PARTS):
        for way in range(2):
            wd_direct(p, way).wait_send()
            wd_relay(p, way).wait_send()
            wd_hand(p, way, mine).wait_send()
            wd_hand_relayed(p, way, mine).wait_send()

    def sent(e, carry):
        b, _, used, ways = event(e)

        @pl.when(jnp.logical_and(used, e > 0))
        def _():
            sib_copy(b).wait_send()

        for way in range(3):
            @pl.when(ways[way])
            def _():
                kv_copy(b, way).wait_send()

        return carry

    lax.fori_loop(0, 16, sent, 0)

    for copy in ctx_copies:
        copy.wait_send()
    for n in range(QROWS):
        @pl.when(jnp.logical_not(is_self(n)))
        def _():
            row_copy(n).wait_send()

    write.wait()
    own_out.wait()
    for n, tp in enumerate((topp, tn, tb)):
        out_copies[n].wait_send()
    for tp in (topp, tn, tb):
        remote(osend.at[0], out_rows(tp), out_send.at[0], out_recv.at[tp], tp=tp).wait_recv()


def hand_on(temporal_in, depth_in, temporal_out, depth_out):
    temporal_out[...] = temporal_in[...]
    depth_out[...] = depth_in[...]


def body(
    frames, w_query, w_key, w_value, w_out, frame_pick, codes, geo_ids, geo_table, w_context, code_table,
    level_table, wd_query, wd_key, wd_value, wd_out,
):
    hbm = pl.BlockSpec(memory_space=pl.ANY)
    vmem = pl.BlockSpec(memory_space=pltpu.VMEM)
    sem = pltpu.SemaphoreType.DMA
    temporal, depth = pl.pallas_call(
        kernel,
        out_shape=(
            jax.ShapeDtypeStruct((ROWS, 512), BF16),
            jax.ShapeDtypeStruct((SEQ * LEVELS, 256), BF16),
        ),
        in_specs=[hbm, hbm, hbm, hbm, hbm, vmem, vmem, vmem, vmem, hbm, hbm, vmem, hbm, hbm, hbm, hbm],
        out_specs=(hbm, hbm),
        scratch_shapes=[
            pltpu.VMEM((ROWS, D), BF16),
            pltpu.VMEM((ROWS, D), BF16),
            pltpu.VMEM((D, 1024), BF16),
            pltpu.VMEM((2, ROWS, 256), BF16),
            pltpu.VMEM((4, ROWS, HEAD), BF16),
            pltpu.VMEM((4, ROWS, HEAD), BF16),
            pltpu.VMEM((CHIPS, PAIR, 256), BF16),
            pltpu.VMEM((2, 1, PAIR), F32),
            pltpu.VMEM((2, 1, PAIR), F32),
            pltpu.VMEM((2, HEAD, PAIR), F32),
            pltpu.VMEM((4, ROWS, HEAD), BF16),
            pltpu.VMEM((TP, ROWS, 512), BF16),
            pltpu.VMEM((D, 512), BF16),
            pltpu.VMEM((ROWS, 512), BF16),
            pltpu.VMEM((512, DD), BF16),
            pltpu.VMEM((SEQ, 8, 128), F32),
            pltpu.VMEM((TP, QROWS, 8, 128), F32),
            pltpu.VMEM((QROWS, 8, 128), F32),
            pltpu.VMEM((QROWS, 8, 128), F32),
            pltpu.VMEM((DD, DD), BF16),
            pltpu.VMEM((TP, 3, DD, 256), BF16),
            pltpu.VMEM((DD, DD), BF16),
            pltpu.VMEM((DROWS, DD), F32),
            pltpu.VMEM((DROWS, DD), BF16),
            pltpu.VMEM((DROWS, DD), BF16),
            pltpu.VMEM((TP, DROWS, 256), BF16),
            sem((13,)),
            sem((5,)),
            sem((4,)),
            sem((3, CHIPS)),
            sem((CHIPS,)),
            sem((CHIPS,)),
            sem((CHIPS,)),
            sem((6,)),
            sem((8,)),
            sem((4, 8)),
            sem((4, 8)),
            sem((15,)),
            sem((TP, 4)),
            sem((3,)),
            sem((TP,)),
            sem((QROWS,)),
            sem((QROWS,)),
            sem((3,)),
            sem((TP,)),
            sem(()),
        ],
        compiler_params=pltpu.CompilerParams(
            collective_id=0, has_side_effects=True, vmem_limit_bytes=58 * 1024 * 1024
        ),
        name="codec_layers",
    )(
        frames, w_query, w_key, w_value, w_out, frame_pick.reshape(1, SEQ), codes, geo_ids.reshape(1, SEQ),
        geo_table, w_context, code_table, level_table, wd_query, wd_key, wd_value, wd_out,
    )
    temporal, depth = pl.pallas_call(
        hand_on,
        out_shape=(
            jax.ShapeDtypeStruct((ROWS, 512), BF16),
            jax.ShapeDtypeStruct((SEQ * LEVELS, 256), BF16),
        ),
        in_specs=[vmem, vmem],
        out_specs=(vmem, vmem),
        compiler_params=pltpu.CompilerParams(vmem_limit_bytes=58 * 1024 * 1024),
        name="hand_on",
    )(temporal, depth)
    return temporal, depth.reshape(SEQ, LEVELS, 256)


def solution(mesh):
    return jax.shard_map(
        body,
        mesh=mesh,
        in_specs=(
            P(("dp", "seq"), None),
            P(None, "tp"),
            P(None, "tp"),
            P(None, "tp"),
            P("tp", None),
            P(("dp", "seq"), None, None),
            P(("dp", "seq"), None),
            P(("dp", "seq")),
            P(),
            P("tp", None),
            P(),
            P(),
            P(None, "tp"),
            P(None, "tp"),
            P(None, "tp"),
            P("tp", None),
        ),
        out_specs=(P(("dp", "seq"), "tp"), P(("dp", "seq"), None, "tp")),
        check_vma=False,
    )
```

```python
import functools
import math

import jax
import jax.numpy as jnp
from jax import lax
from jax.experimental import pallas as pl
from jax.experimental.pallas import tpu as pltpu
from jax.sharding import PartitionSpec as P

MESH = pl.DeviceIdType.MESH
BF16 = jnp.bfloat16
F32 = jnp.float32
LOG2E = math.log2(math.e)

ROWS = 256
D = 2048
HEAD = 128
DD = 1024
DHEAD = 64
LEVELS = 32
SEQ = 32
TP = 4
CHIPS = 16
PAIR = 2 * ROWS
QROWS = 8
DROWS = QROWS * LEVELS
NEG = -1e30

GROUPS = (
    (((0, 0),), ((0, 1), (1, 0)), ((1, 1), (0, 2)), (), ((0, 3),), (), ()),
    (((1, 0),), ((1, 1), (0, 0)), ((0, 1), (1, 2)), ((0, 2),), ((1, 3),), ((0, 3),), ()),
    (
        ((2, 0),), ((2, 1), (1, 0)), ((1, 1), (0, 0), (2, 2)), ((1, 2), (0, 1)), ((0, 2), (2, 3)), ((1, 3),),
        ((0, 3),),
    ),
    (
        ((3, 0),), ((3, 1), (2, 0), (0, 0)), ((2, 1), (0, 1), (3, 2)), ((2, 2), (1, 0)), ((1, 2), (1, 1), (3, 3)),
        ((2, 3), (0, 2)), ((1, 3), (0, 3)),
    ),
)
ORDER = tuple(tuple(z ^ k for k in range(4)) for z in range(4))
ACROSS, UP, DOWN = range(3)


def event_fields(y, z, group, n):
    if n >= len(GROUPS[y][group]):
        return 0
    br, k = GROUPS[y][group][n]
    bz = ORDER[z][k]
    if br == 3 and bz // 2 > z // 2:
        return 0
    row = br == y
    across = row and k < 2 and (y < 3 or z < 2)
    up = (row and y < 3) or (y == 1 and br == 0 and k >= 2) or (y == 2 and br == 1 and k >= 2)
    down = (row and (y == 0 or (y == 1 and k < 2))) or (y == 0 and br == 1) or (y == 3 and br == 0 and k < 2)
    used = br < y or (row and bz // 2 <= z // 2)
    bits = br * 4 + bz
    for place, flag in enumerate((True, used, across, up, down)):
        bits += int(flag) << (4 + place)
    return bits


EVENT_WORDS = tuple(
    tuple(sum(event_fields(n // 4, n % 4, w, i) << (10 * i) for i in range(3)) for n in range(CHIPS))
    for w in range(7)
)


def pick(index, values):
    out = jnp.int32(values[0]) if isinstance(values[0], int) else values[0]
    for place, value in enumerate(values[1:], 1):
        out = jnp.where(index == place, jnp.int32(value) if isinstance(value, int) else value, out)
    return out


def dot(a, b):
    return jnp.dot(a, b, preferred_element_type=F32)


def dot_nt(a, b):
    return lax.dot_general(a, b, (((1,), (1,)), ((), ())), preferred_element_type=F32)


def dot_tn(a, b):
    return lax.dot_general(a, b, (((0,), (0,)), ((), ())), preferred_element_type=F32)


def kernel(
    frames_h, wq_h, wk_h, wv_h, wo_h, pick_ref, codes_ref, geo_ref, geot_ref, wc_h, codet_h, level_ref,
    wdq_h, wdk_h, wdv_h, wdo_h,
    temporal_h, depth_h,
    frames, normed, wqkv, kv_st, q_st, q_all, kv, m_s, l_s, acc_s, att_st, att, far_st, far_in, near_st, near_in, wo, temporal, wc, ctx_st, ctx_in, ctx_mine, ctx_rv,
    codet, wall, wdo, hid, dn, datt, osend,
    load_sem, d2d_send, q_recv, kv_send, kv_recv, sib_send, sib_recv, wd_send, wd_recv, att_send, att_recv, sum_send, sum_recv,
    ctx_send, ctx_recv, row_send, row_recv, out_send, out_recv, self_sem,
):
    s = lax.axis_index("seq")
    t = lax.axis_index("tp")
    y = s // 8
    z = (s // 2) % 4
    c = s % 2
    chip = s // 2
    sib = s + 1 - 2 * c
    tn = (t + 1) % TP
    tb = (t + 3) % TP
    topp = (t + 2) % TP
    half = pl.multiple_of(c * ROWS, ROWS)

    def remote(src, dst, ssem, rsem, seq=None, tp=None):
        return pltpu.make_async_remote_copy(
            src_ref=src, dst_ref=dst, send_sem=ssem, recv_sem=rsem,
            device_id={"seq": s if seq is None else seq, "tp": t if tp is None else tp},
            device_id_type=MESH,
        )

    loads = [
        pltpu.make_async_copy(frames_h, frames, load_sem.at[0]),
        pltpu.make_async_copy(wk_h, wqkv.at[:, 0:256], load_sem.at[1]),
        pltpu.make_async_copy(wv_h, wqkv.at[:, 256:512], load_sem.at[2]),
        pltpu.make_async_copy(wq_h, wqkv.at[:, 512:1024], load_sem.at[3]),
        pltpu.make_async_copy(wdq_h, wall.at[t, 0], load_sem.at[4]),
        pltpu.make_async_copy(wdk_h, wall.at[t, 1], load_sem.at[5]),
        pltpu.make_async_copy(wdv_h, wall.at[t, 2], load_sem.at[6]),
        pltpu.make_async_copy(wdo_h, wdo.at[pl.ds(pl.multiple_of(t * 256, 256), 256), :], load_sem.at[7]),
        pltpu.make_async_copy(wo_h, wo, load_sem.at[8]),
        pltpu.make_async_copy(wc_h, wc, load_sem.at[9]),
        pltpu.make_async_copy(codet_h, codet, load_sem.at[10]),
    ]
    for load in loads:
        load.start()

    barrier = pltpu.get_barrier_semaphore()

    def greet(seq, tp):
        pl.semaphore_signal(barrier, inc=1, device_id={"seq": seq, "tp": tp}, device_id_type=MESH)

    p = z % 2
    op = 1 - p
    mate = s + 2 * (1 - 2 * p)
    mate_sib = sib + 2 * (1 - 2 * p)
    seq_of = (s + 4 * (1 - 2 * (z // 2)), ((y + 1) % 4) * 8 + s % 8, ((y + 3) % 4) * 8 + s % 8)
    greet(sib, t)
    greet(mate, t)
    greet(mate_sib, t)
    for way in range(3):
        greet(seq_of[way], t)
    for tp in (tn, tb):
        greet(s, tp)
        greet(sib, tp)
    greet(s, topp)

    for n in range(QROWS):
        @pl.when(jnp.logical_not(jnp.logical_and(t * 8 + n == s, s // 8 == t)))
        def _():
            greet(t * 8 + n, s // 8)

    loads[0].wait()
    for r in range(4):
        rows = pl.ds(r * 64, 64)
        x = frames[rows, :].astype(F32)
        normed[rows, :] = (x * lax.rsqrt(jnp.mean(x * x, axis=-1, keepdims=True) + 1e-05)).astype(BF16)
    loads[1].wait()
    both = dot(normed[...], wqkv[:, 0:256]).astype(BF16)
    kv_st[0, :, 0:128] = both[:, 0:128]
    kv_st[1, :, 0:128] = both[:, 128:256]
    loads[2].wait()
    both = dot(normed[...], wqkv[:, 256:512]).astype(BF16)
    kv_st[0, :, 128:256] = both[:, 0:128]
    kv_st[1, :, 128:256] = both[:, 128:256]

    own_part = jnp.where(s // 8 == t, 1, 0)
    pl.semaphore_wait(barrier, 6 + 5 + QROWS - own_part)

    oc = 1 - c
    my_rows = pl.ds(half, ROWS)
    other_rows = pl.ds(pl.multiple_of(oc * ROWS, ROWS), ROWS)

    def kv_half(b, rows):
        return kv.at[b, rows, :]

    kv_mate = remote(kv_st.at[op], kv_half(chip, my_rows), d2d_send.at[0], kv_recv.at[chip], seq=mate)
    kv_sib = remote(kv_st.at[p], kv_half(chip, my_rows), d2d_send.at[1], sib_recv.at[chip], seq=sib)
    kv_mate.start()
    kv_sib.start()
    kv[chip, my_rows, :] = kv_st[p]

    def kv_copy(b, way):
        return remote(kv_half(b, my_rows), kv_half(b, my_rows), kv_send.at[way, b], kv_recv.at[b], seq=seq_of[way])

    def sib_copy(b):
        return remote(kv_half(b, my_rows), kv_half(b, my_rows), sib_send.at[b], sib_recv.at[b], seq=sib)

    def forward(b, ways):
        for way in (DOWN, UP, ACROSS):
            @pl.when(ways[way])
            def _():
                kv_copy(b, way).start()

    words = [pick(chip, table) for table in EVENT_WORDS]

    def event(word, n):
        bits = word // (1024**n)
        flags = [(bits // (16 << i)) % 2 == 1 for i in range(5)]
        return bits % 16, flags[0], flags[1], flags[2:]

    first_block, _, _, first_ways = event(words[0], 0)
    forward(first_block, first_ways)

    q_slot = p * 2 + c

    def q_copy(n, seq, head):
        return remote(q_st.at[head], q_all.at[q_slot], d2d_send.at[2 + n], q_recv.at[q_slot], seq=seq)

    q_copies = [
        q_copy(0, mate, op * 2 + c), q_copy(1, mate_sib, op * 2 + oc), q_copy(2, sib, p * 2 + oc),
    ]

    def square_part(m):
        def part(tp, lo, n):
            return wall.at[tp, m, pl.ds(pl.multiple_of(lo * 4, 256), n * 4), :]

        return part

    def out_part(tp, lo, n):
        return wdo.at[pl.ds(pl.multiple_of(tp * 256 + lo, 64), n), :]

    parts = (square_part(0), square_part(1), square_part(2), out_part)
    PARTS = len(parts)
    mine = c * 128
    theirs = oc * 128

    def wd_direct(p, way):
        if p < 3:
            src = (wdq_h, wdk_h, wdv_h)[p].at[pl.ds(pl.multiple_of(mine * 4, 512), 512), :]
        else:
            src = wdo_h.at[pl.ds(pl.multiple_of(mine, 128), 128), :]
        return remote(src, parts[p](t, mine, 128), wd_send.at[p, way], wd_recv.at[p, way], tp=(tn, tb)[way])

    def wd_start(p):
        for way in range(2):
            wd_direct(p, way).start()

    def wd_first():
        wd_start(0)
        wd_start(1)

    def wd_relay(p, way):
        tp = (tb, tn)[way]
        ref = parts[p](tp, mine + way * 64, 64)
        return remote(ref, ref, wd_send.at[p, 2 + way], wd_recv.at[p, 2 + way], tp=(tn, tb)[way])

    def wd_hand(p, way, core_lo):
        tp = (tb, tn)[way]
        ref = parts[p](tp, core_lo, 128)
        return remote(ref, ref, wd_send.at[p, 4 + way], wd_recv.at[p, 4 + way], seq=sib)

    def wd_hand_relayed(p, way, core_lo):
        ref = parts[p](topp, core_lo + way * 64, 64)
        return remote(ref, ref, wd_send.at[p, 6 + way], wd_recv.at[p, 6 + way], seq=sib)

    def wd_direct_arrived(p, way):
        ref = parts[p]((tb, tn)[way], mine, 128)
        return remote(ref, ref, wd_send.at[p, way], wd_recv.at[p, way], tp=(tn, tb)[way])

    def wd_relay_arrived(p, way):
        ref = parts[p](topp, mine + way * 64, 64)
        return remote(ref, ref, wd_send.at[p, 2 + way], wd_recv.at[p, 2 + way], tp=(tn, tb)[way])

    def wd_pass_relayed(p):
        for way in range(2):
            wd_relay_arrived(p, way).wait_recv()
            wd_hand_relayed(p, way, mine).start()

    def wd_pass(p):
        for way in range(2):
            wd_direct_arrived(p, way).wait_recv()
            wd_relay(p, way).start()
            wd_hand(p, way, mine).start()

    wd_first()
    loads[3].wait()
    scale = HEAD ** (-0.5) * LOG2E
    for n in range(2):
        both = (dot(normed[...], wqkv[:, 512 + n * 256 : 768 + n * 256]) * scale).astype(BF16)
        q_st[2 * n] = both[:, 0:128]
        q_st[2 * n + 1] = both[:, 128:256]
    for copy in q_copies:
        copy.start()
    q_all[q_slot] = q_st[q_slot]


    for h in range(2):
        m_s[h] = jnp.full((1, PAIR), NEG, F32)
        l_s[h] = jnp.zeros((1, PAIR), F32)
        acc_s[h] = jnp.zeros((HEAD, PAIR), F32)

    def fold(b, masked):
        for h in range(2):
            keys = kv[b, :, 0:128]
            values = kv[b, :, 128:256]
            queries = q_all[2 * h : 2 * h + 2].reshape(PAIR, HEAD)
            scores = dot_nt(keys, queries)
            if masked:
                ahead = (b - (chip // 2 * 2 + h)) * PAIR
                kpos = lax.broadcasted_iota(jnp.int32, (PAIR, PAIR), 0) + ahead
                qpos = lax.broadcasted_iota(jnp.int32, (PAIR, PAIR), 1)
                scores = jnp.where(kpos <= qpos, scores, NEG)
            old = m_s[h]
            top = jnp.maximum(old, jnp.max(scores, axis=0, keepdims=True))
            weights = jnp.exp2(scores - top)
            factor = jnp.exp2(old - top)
            l_s[h] = l_s[h] * factor + jnp.sum(weights, axis=0, keepdims=True)
            acc_s[h] = acc_s[h] * factor + dot_tn(values, weights.astype(BF16))
            m_s[h] = top

    def fold_arrived(b, used):
        @pl.when(used)
        def _():
            remote(
                kv_half(b, other_rows), kv_half(b, other_rows), sib_send.at[b], sib_recv.at[b], seq=sib
            ).wait_recv()

        masked = b // 2 == chip // 2

        @pl.when(jnp.logical_and(used, masked))
        def _():
            fold(b, True)

        @pl.when(jnp.logical_and(used, jnp.logical_not(masked)))
        def _():
            fold(b, False)

    for head in range(4):
        @pl.when(head != q_slot)
        def _():
            remote(q_all.at[head], q_all.at[head], d2d_send.at[0], q_recv.at[head], seq=sib).wait_recv()

    def step(w, carry):
        word = pick(w, words)
        for n in range(3):
            b, valid, used, ways = event(word, n)

            @pl.when(jnp.logical_and(valid, w > 0))
            def _():
                kv_copy(b, UP).wait_recv()
                forward(b, ways)

            @pl.when(jnp.logical_and(used, w > 0))
            def _():
                sib_copy(b).start()

        def fold_one(n, carry):
            bits = jnp.where(n == 0, word, jnp.where(n == 1, word // 1024, word // (1024 * 1024)))
            fold_arrived(bits % 16, (bits // 32) % 2 == 1)
            return carry

        lax.fori_loop(0, 3, fold_one, 0)

        @pl.when(w == 2)
        def _():
            wd_pass(0)
            wd_start(2)

        @pl.when(w == 4)
        def _():
            wd_pass(1)
            wd_start(3)

        return carry

    lax.fori_loop(0, 7, step, 0)

    my_lanes = pl.ds(pl.multiple_of(q_slot * HEAD, HEAD), HEAD)

    def att_copy(n, group, seq):
        return remote(att_st.at[group], att.at[:, my_lanes], att_send.at[n], att_recv.at[q_slot], seq=seq)

    att_copies = [
        att_copy(0, op * 2 + c, mate), att_copy(1, op * 2 + oc, mate_sib), att_copy(2, p * 2 + oc, sib),
    ]
    for h in range(2):
        heads = acc_s[h] / l_s[h]
        heads = heads * lax.rsqrt(jnp.mean(heads * heads, axis=0, keepdims=True) + 1e-06)
        heads = heads.T.astype(BF16)
        att_st[2 * h] = heads[0:256]
        att_st[2 * h + 1] = heads[256:512]
    for copy in att_copies:
        copy.start()
    att[:, my_lanes] = att_st[q_slot]

    loads[10].wait()
    row_level = lax.broadcasted_iota(jnp.int32, (DROWS, LEVELS), 0) % LEVELS
    lane = lax.broadcasted_iota(jnp.int32, (DROWS, LEVELS), 1)
    my_codes = codes_ref[pl.ds(pl.multiple_of(t * QROWS, QROWS), QROWS), :]
    spread = jnp.broadcast_to(my_codes[:, None, :], (QROWS, LEVELS, LEVELS)).reshape(DROWS, LEVELS)
    code = jnp.sum(jnp.where(lane == row_level - 1, spread, 0), axis=-1, keepdims=True)
    level0 = lax.broadcasted_iota(jnp.int32, (DROWS, 1), 0) % LEVELS == 0
    code = jnp.where(level0, -1, code)
    slab_row = lax.broadcasted_iota(jnp.int32, (DROWS, LEVELS), 0) // LEVELS + t * QROWS
    geo = jnp.sum(jnp.where(lane == slab_row, jnp.broadcast_to(geo_ref[...], (DROWS, LEVELS)), 0), axis=-1, keepdims=True)
    code_hot = (lax.broadcasted_iota(jnp.int32, (DROWS, DD), 1) == code).astype(F32).astype(BF16)
    geo_hot = (lax.broadcasted_iota(jnp.int32, (DROWS, 64), 1) == geo).astype(F32).astype(BF16)
    for n in range(4):
        part = slice(n * 256, (n + 1) * 256)
        level = jnp.broadcast_to(level_ref[:, part].astype(F32)[None], (QROWS, LEVELS, 256)).reshape(DROWS, 256)
        hid[:, part] = dot(code_hot, codet[:, part]) + dot(geo_hot, geot_ref[:, part]) + level

    loads[8].wait()
    for head in range(4):
        @pl.when(head != q_slot)
        def _():
            ref = att.at[:, head * HEAD : (head + 1) * HEAD]
            remote(ref, ref, att_send.at[0], att_recv.at[head], seq=sib).wait_recv()

    def project(tp):
        return dot(att[...], wo[:, pl.ds(pl.multiple_of(tp * 512, 512), 512)])

    def far_copy(way):
        return remote(far_st.at[way], far_in.at[way], sum_send.at[way], sum_recv.at[way], tp=(tn, tb)[way])

    def near_copy(way, part):
        n = 2 + 2 * way + part
        return remote(
            near_st.at[way, part], near_in.at[way, part], sum_send.at[n], sum_recv.at[n], tp=(tn, tb)[way]
        )

    far = project(topp).astype(BF16)
    for way in range(2):
        far_st[way] = far[way * 128 : way * 128 + 128]
        far_copy(way).start()
    near = [project(tn), project(tb)]
    near_st[0, 1] = near[0][128:256].astype(BF16)
    near_copy(0, 1).start()
    near_st[1, 0] = near[1][0:128].astype(BF16)
    near_copy(1, 0).start()
    total = frames[:, pl.ds(pl.multiple_of(t * 512, 512), 512)].astype(F32) + project(t)
    for way in range(2):
        far_copy(way).wait_recv()
        passing = near[way][way * 128 : way * 128 + 128] + far_in[way].astype(F32)
        near_st[way, way] = passing.astype(BF16)
        near_copy(way, way).start()
    for way in range(2):
        for part in range(2):
            near_copy(way, part).wait_recv()
    total += near_in[0].reshape(ROWS, 512).astype(F32) + near_in[1].reshape(ROWS, 512).astype(F32)
    temporal[...] = total.astype(BF16)
    write = pltpu.make_async_copy(temporal, temporal_h, load_sem.at[11])
    write.start()

    wd_pass(2)

    loads[9].wait()
    pick_hot = (lax.broadcasted_iota(jnp.int32, (ROWS, SEQ), 0) == pick_ref[...]).astype(F32).astype(BF16)
    picked = dot_tn(pick_hot, temporal[...]).astype(BF16)
    for n in range(8):
        ctx_st[:, n, :] = dot(picked, wc[:, n * 128 : (n + 1) * 128])
    def ctx_rows(u):
        return ctx_st.at[pl.ds(pl.multiple_of(u * QROWS, QROWS), QROWS)]

    def ctx_copy(n, tp):
        return remote(ctx_rows(tp), ctx_in.at[t], ctx_send.at[n], ctx_recv.at[t], tp=tp)

    ctx_copies = [ctx_copy(n, tp) for n, tp in enumerate((topp, tn, tb))]
    for copy in ctx_copies:
        copy.start()

    wd_pass_relayed(0)
    wd_pass_relayed(1)
    wd_pass(3)

    ctx_total = ctx_st[pl.ds(pl.multiple_of(t * QROWS, QROWS), QROWS)].astype(BF16).astype(F32)
    for tp in (tn, tb, topp):
        remote(ctx_in.at[tp], ctx_in.at[tp], ctx_send.at[0], ctx_recv.at[tp], tp=tp).wait_recv()
        ctx_total = ctx_total + ctx_in[tp].astype(BF16).astype(F32)
    ctx_mine[...] = ctx_total.astype(BF16).astype(F32)

    to_tp = s // 8
    stays = to_tp == t
    place = s % 8

    def row_copy(n):
        return remote(ctx_mine.at[n], ctx_rv.at[place], row_send.at[n], row_recv.at[place], seq=t * 8 + n, tp=to_tp)

    def is_self(n):
        return jnp.logical_and(t * 8 + n == s, stays)

    for n in range(QROWS):
        @pl.when(jnp.logical_not(is_self(n)))
        def _():
            row_copy(n).start()

    own_row = pltpu.make_async_copy(ctx_mine.at[place], ctx_rv.at[place], self_sem)

    @pl.when(stays)
    def _():
        own_row.start()
        own_row.wait()

    for n in range(QROWS):
        @pl.when(jnp.logical_not(is_self(n)))
        def _():
            ref = ctx_rv.at[n]
            remote(ref, ref, row_send.at[n], row_recv.at[n], seq=sib).wait_recv()

    for load in loads[4:8]:
        load.wait()

    square = jnp.zeros((DROWS, 1), F32)
    for n in range(8):
        part = slice(n * 128, (n + 1) * 128)
        rows = []
        for r in range(QROWS):
            rows.append(jnp.broadcast_to(ctx_rv[r, n : n + 1, :], (LEVELS, 128)))
        value = hid[:, part] + jnp.concatenate(rows, axis=0)
        hid[:, part] = value
        square += jnp.sum(value * value, axis=-1, keepdims=True)
    factor = lax.rsqrt(square * (1.0 / DD) + 1e-05)
    dn[...] = (hid[...] * factor).astype(BF16)

    dscale = DHEAD ** (-0.5) * LOG2E
    lrow = lax.broadcasted_iota(jnp.int32, (128, 128), 0)
    lcol = lax.broadcasted_iota(jnp.int32, (128, 128), 1)
    allowed = jnp.logical_and(lrow // LEVELS == lcol // LEVELS, lrow <= lcol)

    for n, g in enumerate((t, tb, tn, topp)):
        if n == 1 or n == 2:
            for p in range(3):
                wd_hand(p, n - 1, theirs).wait_recv()
        if n == 1:
            wd_pass_relayed(2)
        if n == 3:
            wd_pass_relayed(3)
        if n == 3:
            for p in range(3):
                for way in range(2):
                    wd_hand_relayed(p, way, theirs).wait_recv()
        queries = (dot(dn[...], wall[g, 0]) * dscale).astype(BF16)
        keys = dot(dn[...], wall[g, 1]).astype(BF16)
        values = dot(dn[...], wall[g, 2]).astype(BF16)
        for r in range(2):
            rows = slice(r * 128, (r + 1) * 128)
            outs = []
            for h in range(4):
                part = slice(h * DHEAD, (h + 1) * DHEAD)
                scores = dot_nt(keys[rows, part], queries[rows, part])
                scores = jnp.where(allowed, scores, NEG)
                top = jnp.max(scores, axis=0, keepdims=True)
                weights = jnp.exp2(scores - top)
                sums = jnp.sum(weights, axis=0, keepdims=True)
                heads = dot_tn(values[rows, part], weights.astype(BF16)) / sums
                heads = heads * lax.rsqrt(jnp.mean(heads * heads, axis=0, keepdims=True) + 1e-06)
                outs.append(heads)
            datt[rows, pl.ds(pl.multiple_of(g * 256, 256), 256)] = jnp.concatenate(outs, axis=0).T.astype(BF16)

    for way in range(2):
        wd_hand(3, way, theirs).wait_recv()
        wd_hand_relayed(3, way, theirs).wait_recv()

    def out_tile(tp):
        part = pl.ds(pl.multiple_of(tp * 256, 256), 256)
        return (dot(datt[...], wdo[:, part]) + hid[:, part]).astype(BF16)

    def out_rows(tp):
        return depth_h.at[pl.ds(pl.multiple_of(tp * DROWS, DROWS), DROWS), :]

    out_copies = []
    for n, tp in enumerate((topp, tn, tb)):
        osend[n] = out_tile(tp)
        copy = remote(osend.at[n], out_rows(t), out_send.at[n], out_recv.at[t], tp=tp)
        copy.start()
        out_copies.append(copy)
    osend[3] = out_tile(t)
    own_out = pltpu.make_async_copy(osend.at[3], out_rows(t), load_sem.at[12])
    own_out.start()

    sums = [far_copy(0), far_copy(1)] + [near_copy(way, part) for way in range(2) for part in range(2)]
    for copy in [kv_mate, kv_sib] + q_copies + att_copies + sums:
        copy.wait_send()
    for p in range(PARTS):
        for way in range(2):
            wd_direct(p, way).wait_send()
            wd_relay(p, way).wait_send()
            wd_hand(p, way, mine).wait_send()
            wd_hand_relayed(p, way, mine).wait_send()

    def sent(w, carry):
        word = pick(w, words)
        for n in range(3):
            b, _, used, ways = event(word, n)

            @pl.when(jnp.logical_and(used, w > 0))
            def _():
                sib_copy(b).wait_send()

            for way in range(3):
                @pl.when(ways[way])
                def _():
                    kv_copy(b, way).wait_send()

        return carry

    lax.fori_loop(0, 7, sent, 0)

    for copy in ctx_copies:
        copy.wait_send()
    for n in range(QROWS):
        @pl.when(jnp.logical_not(is_self(n)))
        def _():
            row_copy(n).wait_send()

    write.wait()
    own_out.wait()
    for n, tp in enumerate((topp, tn, tb)):
        out_copies[n].wait_send()
    for tp in (topp, tn, tb):
        remote(osend.at[0], out_rows(tp), out_send.at[0], out_recv.at[tp], tp=tp).wait_recv()


def hand_on(temporal_in, depth_in, temporal_out, depth_out):
    temporal_out[...] = temporal_in[...]
    depth_out[...] = depth_in[...]


def body(
    frames, w_query, w_key, w_value, w_out, frame_pick, codes, geo_ids, geo_table, w_context, code_table,
    level_table, wd_query, wd_key, wd_value, wd_out,
):
    hbm = pl.BlockSpec(memory_space=pl.ANY)
    vmem = pl.BlockSpec(memory_space=pltpu.VMEM)
    sem = pltpu.SemaphoreType.DMA
    temporal, depth = pl.pallas_call(
        kernel,
        out_shape=(
            jax.ShapeDtypeStruct((ROWS, 512), BF16),
            jax.ShapeDtypeStruct((SEQ * LEVELS, 256), BF16),
        ),
        in_specs=[hbm, hbm, hbm, hbm, hbm, vmem, vmem, vmem, vmem, hbm, hbm, vmem, hbm, hbm, hbm, hbm],
        out_specs=(hbm, hbm),
        scratch_shapes=[
            pltpu.VMEM((ROWS, D), BF16),
            pltpu.VMEM((ROWS, D), BF16),
            pltpu.VMEM((D, 1024), BF16),
            pltpu.VMEM((2, ROWS, 256), BF16),
            pltpu.VMEM((4, ROWS, HEAD), BF16),
            pltpu.VMEM((4, ROWS, HEAD), BF16),
            pltpu.VMEM((CHIPS, PAIR, 256), BF16),
            pltpu.VMEM((2, 1, PAIR), F32),
            pltpu.VMEM((2, 1, PAIR), F32),
            pltpu.VMEM((2, HEAD, PAIR), F32),
            pltpu.VMEM((4, ROWS, HEAD), BF16),
            pltpu.VMEM((ROWS, 512), BF16),
            pltpu.VMEM((2, 128, 512), BF16),
            pltpu.VMEM((2, 128, 512), BF16),
            pltpu.VMEM((2, 2, 128, 512), BF16),
            pltpu.VMEM((2, 2, 128, 512), BF16),
            pltpu.VMEM((512, D), BF16),
            pltpu.VMEM((ROWS, 512), BF16),
            pltpu.VMEM((512, DD), BF16),
            pltpu.VMEM((SEQ, 8, 128), F32),
            pltpu.VMEM((TP, QROWS, 8, 128), F32),
            pltpu.VMEM((QROWS, 8, 128), F32),
            pltpu.VMEM((QROWS, 8, 128), F32),
            pltpu.VMEM((DD, DD), BF16),
            pltpu.VMEM((TP, 3, DD, 256), BF16),
            pltpu.VMEM((DD, DD), BF16),
            pltpu.VMEM((DROWS, DD), F32),
            pltpu.VMEM((DROWS, DD), BF16),
            pltpu.VMEM((DROWS, DD), BF16),
            pltpu.VMEM((TP, DROWS, 256), BF16),
            sem((13,)),
            sem((5,)),
            sem((4,)),
            sem((3, CHIPS)),
            sem((CHIPS,)),
            sem((CHIPS,)),
            sem((CHIPS,)),
            sem((4, 8)),
            sem((4, 8)),
            sem((3,)),
            sem((4,)),
            sem((6,)),
            sem((6,)),
            sem((3,)),
            sem((TP,)),
            sem((QROWS,)),
            sem((QROWS,)),
            sem((3,)),
            sem((TP,)),
            sem(()),
        ],
        compiler_params=pltpu.CompilerParams(
            collective_id=0, has_side_effects=True, vmem_limit_bytes=58 * 1024 * 1024
        ),
        name="codec_layers",
    )(
        frames, w_query, w_key, w_value, w_out, frame_pick.reshape(1, SEQ), codes, geo_ids.reshape(1, SEQ),
        geo_table, w_context, code_table, level_table, wd_query, wd_key, wd_value, wd_out,
    )
    temporal, depth = pl.pallas_call(
        hand_on,
        out_shape=(
            jax.ShapeDtypeStruct((ROWS, 512), BF16),
            jax.ShapeDtypeStruct((SEQ * LEVELS, 256), BF16),
        ),
        in_specs=[vmem, vmem],
        out_specs=(vmem, vmem),
        compiler_params=pltpu.CompilerParams(vmem_limit_bytes=58 * 1024 * 1024),
        name="hand_on",
    )(temporal, depth)
    return temporal, depth.reshape(SEQ, LEVELS, 256)


def solution(mesh):
    return jax.shard_map(
        body,
        mesh=mesh,
        in_specs=(
            P(("dp", "seq"), None),
            P(None, "tp"),
            P(None, "tp"),
            P(None, "tp"),
            P("tp", None),
            P(("dp", "seq"), None, None),
            P(("dp", "seq"), None),
            P(("dp", "seq")),
            P(),
            P("tp", None),
            P(),
            P(),
            P(None, "tp"),
            P(None, "tp"),
            P(None, "tp"),
            P("tp", None),
        ),
        out_specs=(P(("dp", "seq"), "tp"), P(("dp", "seq"), None, "tp")),
        check_vma=False,
    )
```

```python
import functools
import math

import jax
import jax.numpy as jnp
from jax import lax
from jax.experimental import pallas as pl
from jax.experimental.pallas import tpu as pltpu
from jax.sharding import PartitionSpec as P

MESH = pl.DeviceIdType.MESH
BF16 = jnp.bfloat16
F32 = jnp.float32
LOG2E = math.log2(math.e)

ROWS = 256
D = 2048
HEAD = 128
DD = 1024
DHEAD = 64
LEVELS = 32
SEQ = 32
TP = 4
CHIPS = 16
PAIR = 2 * ROWS
QROWS = 8
DROWS = QROWS * LEVELS
NEG = -1e30

GROUPS = (
    (((0, 0),), ((0, 1), (1, 0)), ((1, 1), (0, 2)), (), ((0, 3),), (), ()),
    (((1, 0),), ((1, 1), (0, 0)), ((0, 1), (1, 2)), ((0, 2),), ((1, 3),), ((0, 3),), ()),
    (
        ((2, 0),), ((2, 1), (1, 0)), ((1, 1), (0, 0), (2, 2)), ((1, 2), (0, 1)), ((0, 2), (2, 3)), ((1, 3),),
        ((0, 3),),
    ),
    (
        ((3, 0),), ((3, 1), (2, 0), (0, 0)), ((2, 1), (0, 1), (3, 2)), ((2, 2), (1, 0)), ((1, 2), (1, 1), (3, 3)),
        ((2, 3), (0, 2)), ((1, 3), (0, 3)),
    ),
)
ORDER = tuple(tuple(z ^ k for k in range(4)) for z in range(4))
ACROSS, UP, DOWN = range(3)


def event_fields(y, z, group, n):
    if n >= len(GROUPS[y][group]):
        return 0
    br, k = GROUPS[y][group][n]
    bz = ORDER[z][k]
    if br == 3 and bz // 2 > z // 2:
        return 0
    row = br == y
    across = row and k < 2 and (y < 3 or z < 2)
    up = (row and y < 3) or (y == 1 and br == 0 and k >= 2) or (y == 2 and br == 1 and k >= 2)
    down = (row and (y == 0 or (y == 1 and k < 2))) or (y == 0 and br == 1) or (y == 3 and br == 0 and k < 2)
    used = br < y or (row and bz // 2 <= z // 2)
    bits = br * 4 + bz
    for place, flag in enumerate((True, used, across, up, down)):
        bits += int(flag) << (4 + place)
    return bits


EVENT_WORDS = tuple(
    tuple(sum(event_fields(n // 4, n % 4, w, i) << (10 * i) for i in range(3)) for n in range(CHIPS))
    for w in range(7)
)


def pick(index, values):
    out = jnp.int32(values[0]) if isinstance(values[0], int) else values[0]
    for place, value in enumerate(values[1:], 1):
        out = jnp.where(index == place, jnp.int32(value) if isinstance(value, int) else value, out)
    return out


def dot(a, b):
    return jnp.dot(a, b, preferred_element_type=F32)


def dot_nt(a, b):
    return lax.dot_general(a, b, (((1,), (1,)), ((), ())), preferred_element_type=F32)


def dot_tn(a, b):
    return lax.dot_general(a, b, (((0,), (0,)), ((), ())), preferred_element_type=F32)


def kernel(
    frames_h, wq_h, wk_h, wv_h, wo_h, pick_ref, codes_ref, geo_ref, geot_ref, wc_h, codet_h, level_ref,
    wdq_h, wdk_h, wdv_h, wdo_h,
    temporal_h, depth_h,
    frames, normed, wqkv, kv_st, q_st, q_all, kv, m_s, l_s, acc_s, att_st, att, far_st, far_in, near_st, near_in, wo, temporal, wc, ctx_st, ctx_in, ctx_mine, ctx_rv,
    codet, wall, wdo, hid, dn, datt, osend,
    load_sem, d2d_send, q_recv, kv_send, kv_recv, sib_send, sib_recv, wd_send, wd_recv, att_send, att_recv, sum_send, sum_recv,
    ctx_send, ctx_recv, row_send, row_recv, out_send, out_recv, self_sem,
):
    s = lax.axis_index("seq")
    t = lax.axis_index("tp")
    y = s // 8
    z = (s // 2) % 4
    c = s % 2
    chip = s // 2
    sib = s + 1 - 2 * c
    tn = (t + 1) % TP
    tb = (t + 3) % TP
    topp = (t + 2) % TP
    half = pl.multiple_of(c * ROWS, ROWS)

    def remote(src, dst, ssem, rsem, seq=None, tp=None):
        return pltpu.make_async_remote_copy(
            src_ref=src, dst_ref=dst, send_sem=ssem, recv_sem=rsem,
            device_id={"seq": s if seq is None else seq, "tp": t if tp is None else tp},
            device_id_type=MESH,
        )

    loads = [
        pltpu.make_async_copy(frames_h, frames, load_sem.at[0]),
        pltpu.make_async_copy(wk_h, wqkv.at[:, 0:256], load_sem.at[1]),
        pltpu.make_async_copy(wv_h, wqkv.at[:, 256:512], load_sem.at[2]),
        pltpu.make_async_copy(wq_h, wqkv.at[:, 512:1024], load_sem.at[3]),
        pltpu.make_async_copy(wdq_h, wall.at[t, 0], load_sem.at[4]),
        pltpu.make_async_copy(wdk_h, wall.at[t, 1], load_sem.at[5]),
        pltpu.make_async_copy(wdv_h, wall.at[t, 2], load_sem.at[6]),
        pltpu.make_async_copy(wdo_h, wdo.at[pl.ds(pl.multiple_of(t * 256, 256), 256), :], load_sem.at[7]),
        pltpu.make_async_copy(wo_h, wo, load_sem.at[8]),
        pltpu.make_async_copy(wc_h, wc, load_sem.at[9]),
        pltpu.make_async_copy(codet_h, codet, load_sem.at[10]),
    ]
    for load in loads:
        load.start()

    barrier = pltpu.get_barrier_semaphore()

    def greet(seq, tp):
        pl.semaphore_signal(barrier, inc=1, device_id={"seq": seq, "tp": tp}, device_id_type=MESH)

    p = z % 2
    op = 1 - p
    mate = s + 2 * (1 - 2 * p)
    mate_sib = sib + 2 * (1 - 2 * p)
    seq_of = (s + 4 * (1 - 2 * (z // 2)), ((y + 1) % 4) * 8 + s % 8, ((y + 3) % 4) * 8 + s % 8)
    greet(sib, t)
    greet(mate, t)
    greet(mate_sib, t)
    for way in range(3):
        greet(seq_of[way], t)
    for tp in (tn, tb):
        greet(s, tp)
        greet(sib, tp)
    greet(s, topp)

    for n in range(QROWS):
        @pl.when(jnp.logical_not(jnp.logical_and(t * 8 + n == s, s // 8 == t)))
        def _():
            greet(t * 8 + n, s // 8)

    loads[0].wait()
    for r in range(4):
        rows = pl.ds(r * 64, 64)
        x = frames[rows, :].astype(F32)
        normed[rows, :] = (x * lax.rsqrt(jnp.mean(x * x, axis=-1, keepdims=True) + 1e-05)).astype(BF16)
    loads[1].wait()
    both = dot(normed[...], wqkv[:, 0:256]).astype(BF16)
    kv_st[0, :, 0:128] = both[:, 0:128]
    kv_st[1, :, 0:128] = both[:, 128:256]
    loads[2].wait()
    both = dot(normed[...], wqkv[:, 256:512]).astype(BF16)
    kv_st[0, :, 128:256] = both[:, 0:128]
    kv_st[1, :, 128:256] = both[:, 128:256]

    own_part = jnp.where(s // 8 == t, 1, 0)
    pl.semaphore_wait(barrier, 6 + 5 + QROWS - own_part)

    oc = 1 - c
    my_rows = pl.ds(half, ROWS)
    other_rows = pl.ds(pl.multiple_of(oc * ROWS, ROWS), ROWS)

    def kv_half(b, rows):
        return kv.at[b, rows, :]

    kv_mate = remote(kv_st.at[op], kv_half(chip, my_rows), d2d_send.at[0], kv_recv.at[chip], seq=mate)
    kv_sib = remote(kv_st.at[p], kv_half(chip, my_rows), d2d_send.at[1], sib_recv.at[chip], seq=sib)
    kv_mate.start()
    kv_sib.start()
    kv[chip, my_rows, :] = kv_st[p]

    def kv_copy(b, way):
        return remote(kv_half(b, my_rows), kv_half(b, my_rows), kv_send.at[way, b], kv_recv.at[b], seq=seq_of[way])

    def sib_copy(b):
        return remote(kv_half(b, my_rows), kv_half(b, my_rows), sib_send.at[b], sib_recv.at[b], seq=sib)

    def forward(b, ways):
        for way in (DOWN, UP, ACROSS):
            @pl.when(ways[way])
            def _():
                kv_copy(b, way).start()

    words = [pick(chip, table) for table in EVENT_WORDS]

    def event(word, n):
        bits = word // (1024**n)
        flags = [(bits // (16 << i)) % 2 == 1 for i in range(5)]
        return bits % 16, flags[0], flags[1], flags[2:]

    first_block, _, _, first_ways = event(words[0], 0)
    forward(first_block, first_ways)

    q_slot = p * 2 + c

    def q_copy(n, seq, head):
        return remote(q_st.at[head], q_all.at[q_slot], d2d_send.at[2 + n], q_recv.at[q_slot], seq=seq)

    q_copies = [
        q_copy(0, mate, op * 2 + c), q_copy(1, mate_sib, op * 2 + oc), q_copy(2, sib, p * 2 + oc),
    ]

    def square_part(m):
        def part(tp, lo, n):
            return wall.at[tp, m, pl.ds(pl.multiple_of(lo * 4, 256), n * 4), :]

        return part

    def out_part(tp, lo, n):
        return wdo.at[pl.ds(pl.multiple_of(tp * 256 + lo, 64), n), :]

    parts = (square_part(0), square_part(1), square_part(2), out_part)
    PARTS = len(parts)
    mine = c * 128
    theirs = oc * 128

    def wd_direct(p, way):
        if p < 3:
            src = (wdq_h, wdk_h, wdv_h)[p].at[pl.ds(pl.multiple_of(mine * 4, 512), 512), :]
        else:
            src = wdo_h.at[pl.ds(pl.multiple_of(mine, 128), 128), :]
        return remote(src, parts[p](t, mine, 128), wd_send.at[p, way], wd_recv.at[p, way], tp=(tn, tb)[way])

    def wd_start(p):
        for way in range(2):
            wd_direct(p, way).start()

    def wd_first():
        wd_start(0)
        wd_start(1)

    def wd_relay(p, way):
        tp = (tb, tn)[way]
        ref = parts[p](tp, mine + way * 64, 64)
        return remote(ref, ref, wd_send.at[p, 2 + way], wd_recv.at[p, 2 + way], tp=(tn, tb)[way])

    def wd_hand(p, way, core_lo):
        tp = (tb, tn)[way]
        ref = parts[p](tp, core_lo, 128)
        return remote(ref, ref, wd_send.at[p, 4 + way], wd_recv.at[p, 4 + way], seq=sib)

    def wd_hand_relayed(p, way, core_lo):
        ref = parts[p](topp, core_lo + way * 64, 64)
        return remote(ref, ref, wd_send.at[p, 6 + way], wd_recv.at[p, 6 + way], seq=sib)

    def wd_direct_arrived(p, way):
        ref = parts[p]((tb, tn)[way], mine, 128)
        return remote(ref, ref, wd_send.at[p, way], wd_recv.at[p, way], tp=(tn, tb)[way])

    def wd_relay_arrived(p, way):
        ref = parts[p](topp, mine + way * 64, 64)
        return remote(ref, ref, wd_send.at[p, 2 + way], wd_recv.at[p, 2 + way], tp=(tn, tb)[way])

    def wd_pass_relayed(p):
        for way in range(2):
            wd_relay_arrived(p, way).wait_recv()
            wd_hand_relayed(p, way, mine).start()

    def wd_pass(p):
        for way in range(2):
            wd_direct_arrived(p, way).wait_recv()
            wd_relay(p, way).start()
            wd_hand(p, way, mine).start()

    wd_first()
    loads[3].wait()
    scale = HEAD ** (-0.5) * LOG2E
    for n in range(2):
        both = (dot(normed[...], wqkv[:, 512 + n * 256 : 768 + n * 256]) * scale).astype(BF16)
        q_st[2 * n] = both[:, 0:128]
        q_st[2 * n + 1] = both[:, 128:256]
    for copy in q_copies:
        copy.start()
    q_all[q_slot] = q_st[q_slot]


    for h in range(2):
        m_s[h] = jnp.full((1, PAIR), NEG, F32)
        l_s[h] = jnp.zeros((1, PAIR), F32)
        acc_s[h] = jnp.zeros((HEAD, PAIR), F32)

    def fold(b, masked):
        for h in range(2):
            keys = kv[b, :, 0:128]
            values = kv[b, :, 128:256]
            queries = q_all[2 * h : 2 * h + 2].reshape(PAIR, HEAD)
            scores = dot_nt(keys, queries)
            if masked:
                ahead = (b - (chip // 2 * 2 + h)) * PAIR
                kpos = lax.broadcasted_iota(jnp.int32, (PAIR, PAIR), 0) + ahead
                qpos = lax.broadcasted_iota(jnp.int32, (PAIR, PAIR), 1)
                scores = jnp.where(kpos <= qpos, scores, NEG)
            old = m_s[h]
            top = jnp.maximum(old, jnp.max(scores, axis=0, keepdims=True))
            weights = jnp.exp2(scores - top)
            factor = jnp.exp2(old - top)
            l_s[h] = l_s[h] * factor + jnp.sum(weights, axis=0, keepdims=True)
            acc_s[h] = acc_s[h] * factor + dot_tn(values, weights.astype(BF16))
            m_s[h] = top

    def fold_arrived(b, used):
        @pl.when(used)
        def _():
            remote(
                kv_half(b, other_rows), kv_half(b, other_rows), sib_send.at[b], sib_recv.at[b], seq=sib
            ).wait_recv()

        masked = b // 2 == chip // 2

        @pl.when(jnp.logical_and(used, masked))
        def _():
            fold(b, True)

        @pl.when(jnp.logical_and(used, jnp.logical_not(masked)))
        def _():
            fold(b, False)

    for head in range(4):
        @pl.when(head != q_slot)
        def _():
            remote(q_all.at[head], q_all.at[head], d2d_send.at[0], q_recv.at[head], seq=sib).wait_recv()

    def step(w, carry):
        word = pick(w, words)
        for n in range(3):
            b, valid, used, ways = event(word, n)

            @pl.when(jnp.logical_and(valid, w > 0))
            def _():
                kv_copy(b, UP).wait_recv()
                forward(b, ways)

            @pl.when(jnp.logical_and(used, w > 0))
            def _():
                sib_copy(b).start()

        def fold_one(n, carry):
            bits = jnp.where(n == 0, word, jnp.where(n == 1, word // 1024, word // (1024 * 1024)))
            fold_arrived(bits % 16, (bits // 32) % 2 == 1)
            return carry

        lax.fori_loop(0, 3, fold_one, 0)

        @pl.when(w == 2)
        def _():
            wd_pass(0)
            wd_start(2)

        @pl.when(w == 4)
        def _():
            wd_pass(1)
            wd_start(3)

        return carry

    lax.fori_loop(0, 7, step, 0)

    my_lanes = pl.ds(pl.multiple_of(q_slot * HEAD, HEAD), HEAD)

    def att_copy(n, group, seq):
        return remote(att_st.at[group], att.at[:, my_lanes], att_send.at[n], att_recv.at[q_slot], seq=seq)

    att_copies = [
        att_copy(0, op * 2 + c, mate), att_copy(1, op * 2 + oc, mate_sib), att_copy(2, p * 2 + oc, sib),
    ]
    for h in range(2):
        heads = acc_s[h] / l_s[h]
        heads = heads * lax.rsqrt(jnp.mean(heads * heads, axis=0, keepdims=True) + 1e-06)
        heads = heads.T.astype(BF16)
        att_st[2 * h] = heads[0:256]
        att_st[2 * h + 1] = heads[256:512]
    for copy in att_copies:
        copy.start()
    att[:, my_lanes] = att_st[q_slot]

    loads[10].wait()
    row_level = lax.broadcasted_iota(jnp.int32, (DROWS, LEVELS), 0) % LEVELS
    lane = lax.broadcasted_iota(jnp.int32, (DROWS, LEVELS), 1)
    my_codes = codes_ref[pl.ds(pl.multiple_of(t * QROWS, QROWS), QROWS), :]
    spread = jnp.broadcast_to(my_codes[:, None, :], (QROWS, LEVELS, LEVELS)).reshape(DROWS, LEVELS)
    code = jnp.sum(jnp.where(lane == row_level - 1, spread, 0), axis=-1, keepdims=True)
    level0 = lax.broadcasted_iota(jnp.int32, (DROWS, 1), 0) % LEVELS == 0
    code = jnp.where(level0, -1, code)
    slab_row = lax.broadcasted_iota(jnp.int32, (DROWS, LEVELS), 0) // LEVELS + t * QROWS
    geo = jnp.sum(jnp.where(lane == slab_row, jnp.broadcast_to(geo_ref[...], (DROWS, LEVELS)), 0), axis=-1, keepdims=True)
    code_hot = (lax.broadcasted_iota(jnp.int32, (DROWS, DD), 1) == code).astype(F32).astype(BF16)
    geo_hot = (lax.broadcasted_iota(jnp.int32, (DROWS, 64), 1) == geo).astype(F32).astype(BF16)
    for n in range(4):
        part = slice(n * 256, (n + 1) * 256)
        level = jnp.broadcast_to(level_ref[:, part].astype(F32)[None], (QROWS, LEVELS, 256)).reshape(DROWS, 256)
        hid[:, part] = dot(code_hot, codet[:, part]) + dot(geo_hot, geot_ref[:, part]) + level

    loads[8].wait()
    for head in range(4):
        @pl.when(head != q_slot)
        def _():
            ref = att.at[:, head * HEAD : (head + 1) * HEAD]
            remote(ref, ref, att_send.at[0], att_recv.at[head], seq=sib).wait_recv()

    def project(tp):
        return dot(att[...], wo[:, pl.ds(pl.multiple_of(tp * 512, 512), 512)])

    def far_copy(way):
        return remote(far_st.at[way], far_in.at[way], sum_send.at[way], sum_recv.at[way], tp=(tn, tb)[way])

    def near_copy(way, part):
        n = 2 + 2 * way + part
        return remote(
            near_st.at[way, part], near_in.at[way, part], sum_send.at[n], sum_recv.at[n], tp=(tn, tb)[way]
        )

    far = project(topp).astype(BF16)
    for way in range(2):
        far_st[way] = far[way * 128 : way * 128 + 128]
        far_copy(way).start()
    near = [project(tn), project(tb)]
    near_st[0, 1] = near[0][128:256].astype(BF16)
    near_copy(0, 1).start()
    near_st[1, 0] = near[1][0:128].astype(BF16)
    near_copy(1, 0).start()
    total = frames[:, pl.ds(pl.multiple_of(t * 512, 512), 512)].astype(F32) + project(t)
    for way in range(2):
        far_copy(way).wait_recv()
        passing = near[way][way * 128 : way * 128 + 128] + far_in[way].astype(F32)
        near_st[way, way] = passing.astype(BF16)
        near_copy(way, way).start()
    wd_pass(2)
    for way in range(2):
        for part in range(2):
            near_copy(way, part).wait_recv()
    total += near_in[0].reshape(ROWS, 512).astype(F32) + near_in[1].reshape(ROWS, 512).astype(F32)
    temporal[...] = total.astype(BF16)
    write = pltpu.make_async_copy(temporal, temporal_h, load_sem.at[11])
    write.start()

    loads[9].wait()
    pick_hot = (lax.broadcasted_iota(jnp.int32, (ROWS, SEQ), 0) == pick_ref[...]).astype(F32).astype(BF16)
    picked = dot_tn(pick_hot, temporal[...]).astype(BF16)
    for n in range(8):
        ctx_st[:, n, :] = dot(picked, wc[:, n * 128 : (n + 1) * 128])
    def ctx_rows(u):
        return ctx_st.at[pl.ds(pl.multiple_of(u * QROWS, QROWS), QROWS)]

    def ctx_copy(n, tp):
        return remote(ctx_rows(tp), ctx_in.at[t], ctx_send.at[n], ctx_recv.at[t], tp=tp)

    ctx_copies = [ctx_copy(n, tp) for n, tp in enumerate((topp, tn, tb))]
    for copy in ctx_copies:
        copy.start()

    wd_pass_relayed(0)
    wd_pass_relayed(1)
    ctx_total = ctx_st[pl.ds(pl.multiple_of(t * QROWS, QROWS), QROWS)].astype(BF16).astype(F32)
    for tp in (tn, tb, topp):
        remote(ctx_in.at[tp], ctx_in.at[tp], ctx_send.at[0], ctx_recv.at[tp], tp=tp).wait_recv()
        ctx_total = ctx_total + ctx_in[tp].astype(BF16).astype(F32)
    ctx_mine[...] = ctx_total.astype(BF16).astype(F32)

    wd_pass(3)

    to_tp = s // 8
    stays = to_tp == t
    place = s % 8

    def row_copy(n):
        return remote(ctx_mine.at[n], ctx_rv.at[place], row_send.at[n], row_recv.at[place], seq=t * 8 + n, tp=to_tp)

    def is_self(n):
        return jnp.logical_and(t * 8 + n == s, stays)

    for n in range(QROWS):
        @pl.when(jnp.logical_not(is_self(n)))
        def _():
            row_copy(n).start()

    own_row = pltpu.make_async_copy(ctx_mine.at[place], ctx_rv.at[place], self_sem)

    @pl.when(stays)
    def _():
        own_row.start()
        own_row.wait()

    for n in range(QROWS):
        @pl.when(jnp.logical_not(is_self(n)))
        def _():
            ref = ctx_rv.at[n]
            remote(ref, ref, row_send.at[n], row_recv.at[n], seq=sib).wait_recv()

    for load in loads[4:8]:
        load.wait()

    square = jnp.zeros((DROWS, 1), F32)
    for n in range(8):
        part = slice(n * 128, (n + 1) * 128)
        rows = []
        for r in range(QROWS):
            rows.append(jnp.broadcast_to(ctx_rv[r, n : n + 1, :], (LEVELS, 128)))
        value = hid[:, part] + jnp.concatenate(rows, axis=0)
        hid[:, part] = value
        square += jnp.sum(value * value, axis=-1, keepdims=True)
    factor = lax.rsqrt(square * (1.0 / DD) + 1e-05)
    dn[...] = (hid[...] * factor).astype(BF16)

    dscale = DHEAD ** (-0.5) * LOG2E
    lrow = lax.broadcasted_iota(jnp.int32, (128, 128), 0)
    lcol = lax.broadcasted_iota(jnp.int32, (128, 128), 1)
    allowed = jnp.logical_and(lrow // LEVELS == lcol // LEVELS, lrow <= lcol)

    for n, g in enumerate((t, tb, tn, topp)):
        if n == 1 or n == 2:
            for p in range(3):
                wd_hand(p, n - 1, theirs).wait_recv()
        if n == 1:
            wd_pass_relayed(2)
        if n == 3:
            wd_pass_relayed(3)
        if n == 3:
            for p in range(3):
                for way in range(2):
                    wd_hand_relayed(p, way, theirs).wait_recv()
        queries = (dot(dn[...], wall[g, 0]) * dscale).astype(BF16)
        keys = dot(dn[...], wall[g, 1]).astype(BF16)
        values = dot(dn[...], wall[g, 2]).astype(BF16)
        for r in range(2):
            rows = slice(r * 128, (r + 1) * 128)
            outs = []
            for h in range(4):
                part = slice(h * DHEAD, (h + 1) * DHEAD)
                scores = dot_nt(keys[rows, part], queries[rows, part])
                scores = jnp.where(allowed, scores, NEG)
                top = jnp.max(scores, axis=0, keepdims=True)
                weights = jnp.exp2(scores - top)
                sums = jnp.sum(weights, axis=0, keepdims=True)
                heads = dot_tn(values[rows, part], weights.astype(BF16)) / sums
                heads = heads * lax.rsqrt(jnp.mean(heads * heads, axis=0, keepdims=True) + 1e-06)
                outs.append(heads)
            datt[rows, pl.ds(pl.multiple_of(g * 256, 256), 256)] = jnp.concatenate(outs, axis=0).T.astype(BF16)

    for way in range(2):
        wd_hand(3, way, theirs).wait_recv()
        wd_hand_relayed(3, way, theirs).wait_recv()

    def out_tile(tp):
        part = pl.ds(pl.multiple_of(tp * 256, 256), 256)
        return (dot(datt[...], wdo[:, part]) + hid[:, part]).astype(BF16)

    def out_rows(tp):
        return depth_h.at[pl.ds(pl.multiple_of(tp * DROWS, DROWS), DROWS), :]

    out_copies = []
    for n, tp in enumerate((topp, tn, tb)):
        osend[n] = out_tile(tp)
        copy = remote(osend.at[n], out_rows(t), out_send.at[n], out_recv.at[t], tp=tp)
        copy.start()
        out_copies.append(copy)
    osend[3] = out_tile(t)
    own_out = pltpu.make_async_copy(osend.at[3], out_rows(t), load_sem.at[12])
    own_out.start()

    sums = [far_copy(0), far_copy(1)] + [near_copy(way, part) for way in range(2) for part in range(2)]
    for copy in [kv_mate, kv_sib] + q_copies + att_copies + sums:
        copy.wait_send()
    for p in range(PARTS):
        for way in range(2):
            wd_direct(p, way).wait_send()
            wd_relay(p, way).wait_send()
            wd_hand(p, way, mine).wait_send()
            wd_hand_relayed(p, way, mine).wait_send()

    def sent(w, carry):
        word = pick(w, words)
        for n in range(3):
            b, _, used, ways = event(word, n)

            @pl.when(jnp.logical_and(used, w > 0))
            def _():
                sib_copy(b).wait_send()

            for way in range(3):
                @pl.when(ways[way])
                def _():
                    kv_copy(b, way).wait_send()

        return carry

    lax.fori_loop(0, 7, sent, 0)

    for copy in ctx_copies:
        copy.wait_send()
    for n in range(QROWS):
        @pl.when(jnp.logical_not(is_self(n)))
        def _():
            row_copy(n).wait_send()

    write.wait()
    own_out.wait()
    for n, tp in enumerate((topp, tn, tb)):
        out_copies[n].wait_send()
    for tp in (topp, tn, tb):
        remote(osend.at[0], out_rows(tp), out_send.at[0], out_recv.at[tp], tp=tp).wait_recv()


def hand_on(temporal_in, depth_in, temporal_out, depth_out):
    temporal_out[...] = temporal_in[...]
    depth_out[...] = depth_in[...]


def body(
    frames, w_query, w_key, w_value, w_out, frame_pick, codes, geo_ids, geo_table, w_context, code_table,
    level_table, wd_query, wd_key, wd_value, wd_out,
):
    hbm = pl.BlockSpec(memory_space=pl.ANY)
    vmem = pl.BlockSpec(memory_space=pltpu.VMEM)
    sem = pltpu.SemaphoreType.DMA
    temporal, depth = pl.pallas_call(
        kernel,
        out_shape=(
            jax.ShapeDtypeStruct((ROWS, 512), BF16),
            jax.ShapeDtypeStruct((SEQ * LEVELS, 256), BF16),
        ),
        in_specs=[hbm, hbm, hbm, hbm, hbm, vmem, vmem, vmem, vmem, hbm, hbm, vmem, hbm, hbm, hbm, hbm],
        out_specs=(hbm, hbm),
        scratch_shapes=[
            pltpu.VMEM((ROWS, D), BF16),
            pltpu.VMEM((ROWS, D), BF16),
            pltpu.VMEM((D, 1024), BF16),
            pltpu.VMEM((2, ROWS, 256), BF16),
            pltpu.VMEM((4, ROWS, HEAD), BF16),
            pltpu.VMEM((4, ROWS, HEAD), BF16),
            pltpu.VMEM((CHIPS, PAIR, 256), BF16),
            pltpu.VMEM((2, 1, PAIR), F32),
            pltpu.VMEM((2, 1, PAIR), F32),
            pltpu.VMEM((2, HEAD, PAIR), F32),
            pltpu.VMEM((4, ROWS, HEAD), BF16),
            pltpu.VMEM((ROWS, 512), BF16),
            pltpu.VMEM((2, 128, 512), BF16),
            pltpu.VMEM((2, 128, 512), BF16),
            pltpu.VMEM((2, 2, 128, 512), BF16),
            pltpu.VMEM((2, 2, 128, 512), BF16),
            pltpu.VMEM((512, D), BF16),
            pltpu.VMEM((ROWS, 512), BF16),
            pltpu.VMEM((512, DD), BF16),
            pltpu.VMEM((SEQ, 8, 128), F32),
            pltpu.VMEM((TP, QROWS, 8, 128), F32),
            pltpu.VMEM((QROWS, 8, 128), F32),
            pltpu.VMEM((QROWS, 8, 128), F32),
            pltpu.VMEM((DD, DD), BF16),
            pltpu.VMEM((TP, 3, DD, 256), BF16),
            pltpu.VMEM((DD, DD), BF16),
            pltpu.VMEM((DROWS, DD), F32),
            pltpu.VMEM((DROWS, DD), BF16),
            pltpu.VMEM((DROWS, DD), BF16),
            pltpu.VMEM((TP, DROWS, 256), BF16),
            sem((13,)),
            sem((5,)),
            sem((4,)),
            sem((3, CHIPS)),
            sem((CHIPS,)),
            sem((CHIPS,)),
            sem((CHIPS,)),
            sem((4, 8)),
            sem((4, 8)),
            sem((3,)),
            sem((4,)),
            sem((6,)),
            sem((6,)),
            sem((3,)),
            sem((TP,)),
            sem((QROWS,)),
            sem((QROWS,)),
            sem((3,)),
            sem((TP,)),
            sem(()),
        ],
        compiler_params=pltpu.CompilerParams(
            collective_id=0, has_side_effects=True, vmem_limit_bytes=58 * 1024 * 1024
        ),
        name="codec_layers",
    )(
        frames, w_query, w_key, w_value, w_out, frame_pick.reshape(1, SEQ), codes, geo_ids.reshape(1, SEQ),
        geo_table, w_context, code_table, level_table, wd_query, wd_key, wd_value, wd_out,
    )
    temporal, depth = pl.pallas_call(
        hand_on,
        out_shape=(
            jax.ShapeDtypeStruct((ROWS, 512), BF16),
            jax.ShapeDtypeStruct((SEQ * LEVELS, 256), BF16),
        ),
        in_specs=[vmem, vmem],
        out_specs=(vmem, vmem),
        compiler_params=pltpu.CompilerParams(vmem_limit_bytes=58 * 1024 * 1024),
        name="hand_on",
    )(temporal, depth)
    return temporal, depth.reshape(SEQ, LEVELS, 256)


def solution(mesh):
    return jax.shard_map(
        body,
        mesh=mesh,
        in_specs=(
            P(("dp", "seq"), None),
            P(None, "tp"),
            P(None, "tp"),
            P(None, "tp"),
            P("tp", None),
            P(("dp", "seq"), None, None),
            P(("dp", "seq"), None),
            P(("dp", "seq")),
            P(),
            P("tp", None),
            P(),
            P(),
            P(None, "tp"),
            P(None, "tp"),
            P(None, "tp"),
            P("tp", None),
        ),
        out_specs=(P(("dp", "seq"), "tp"), P(("dp", "seq"), None, "tp")),
        check_vma=False,
    )
```
